128 devices in a mesh: group: 16 (over z, y), local: 8 (over x, core).
Axes of the slice: x: 4, y: 4, z: 4, core: 2. Of those that a mesh axis runs over, the one named last changes fastest.
Arguments:
- tokens: bfloat16 [16384, 3584], P(('group', 'local')), may hold values from -6 to 6
- expert_ids: int32 [16384, 8], P(('group', 'local')), may hold values from 0 to 127, all different within a row; in each aligned block of 128 rows (0 to 127, 128 to 255, ...) at most 10 rows name the same one
- gate_weights: float32 [16384, 8], P(('group', 'local')), may hold values from 0.05 to 0.5
- w_gate: bfloat16 [128, 3584, 1024], P(('group', 'local')), may hold values from -0.09375 to 0.09375
- w_up: bfloat16 [128, 3584, 1024], P(('group', 'local')), may hold values from -0.09375 to 0.09375
- w_down: bfloat16 [128, 1024, 3584], P(('group', 'local')), may hold values from -0.1875 to 0.1875
Outputs:
- combined: bfloat16 [16384, 3584], P(('group', 'local'))
The draws below stay inside these ranges and needn't reach their ends.
Inputs may be any that keep to these rules, and one draw needn't show every extreme that they name: `expert_ids`: within the rows of one device (aligned blocks of 128 rows) no expert is named by more than 10 rows, and in every draw some expert is named by exactly 10 rows of some device; each row names 8 different experts, and expert e is held by device e of group+local.
All inputs are finite; a program needn't handle non-finite values.
Results may differ from the reference program's by a relative error of at most 0.011.
Values may be sent and summed in bfloat16 or wider, within the bound.
A program may use at most 192 MiB of HBM per device.

```python
import math
import jax
import jax.numpy as jnp
import numpy as np
from jax import lax

D = 3584
H = 1024
TOP = 8
TOK_DEV = 128
EXPERTS = 128
CAP = 10
TOKENS = 16384
N_GROUP = 16
N_LOCAL = 8


def steps_of(key, dims, split, smallest, high):
    loudness, own = 1.0, jax.random.fold_in(key, 6)
    for axis_at, shards_of in split:
        heights = jnp.exp(jax.random.uniform(jax.random.fold_in(own, axis_at), (shards_of,), jnp.float32, smallest / len(split), high / len(split)))
        loudness = loudness * jnp.repeat(heights, dims[axis_at] // shards_of).reshape([-1 if axis == axis_at else 1 for axis in range(len(dims))])
    return loudness


def assign_block(stream_key, own, number, rows, count, top, limit, lean):
    order = jax.random.permutation(stream_key, count)
    crowded, ordinary = load_shares(count, rows * top, limit, lean, True), load_shares(count, rows * top, limit, lean, False)
    places = jnp.arange(count)

    def named(lengths, turn):
        used = int((lengths > 0).sum())
        fixed = max(1, used // 4)
        passed = fixed + (places - fixed + turn * (used - fixed)) % max(1, count - fixed)
        return jnp.zeros((count,), jnp.int32).at[order[jnp.where(places < fixed, places, passed)]].set(jnp.asarray(lengths, jnp.int32))

    lengths = jnp.where(number % 4 == 0, named(crowded, number // 4), named(ordinary, number - number // 4 - 1))
    mixed = jax.random.permutation(jax.random.fold_in(own, 3), count)
    source_of, receiver = mixed[0:count // 2 * 2:2], mixed[1:count // 2 * 2:2]
    slack = jnp.minimum(lengths[source_of] - 1, limit - lengths[receiver]) // 2
    slack = jnp.where((source_of == order[0]) | (receiver == order[0]) | (lengths[receiver] == 0), 0, jnp.maximum(slack, 0))
    passed = jax.random.randint(jax.random.fold_in(own, 4), (count // 2,), 0, 1 << 20) % (slack + 1)
    lengths = lengths.at[source_of].add(-passed).at[receiver].add(passed)
    items = jnp.searchsorted(jnp.cumsum(lengths), jnp.arange(rows * top), side="right").astype(jnp.int32)
    listing = items.reshape(top, rows).T
    listing = listing[jax.random.permutation(jax.random.fold_in(own, 1), rows)]
    turn = jax.random.randint(jax.random.fold_in(own, 2), (rows, 1), 0, top)
    return jnp.take_along_axis(listing, (jnp.arange(top)[None, :] + turn) % top, axis=1)


def load_shares(amount, total, reach, slope, full):
    weights = [(1 << 20) // math.isqrt(standing ** slope) + 1 for standing in range(1, amount + 1)]
    largest = reach if full else min(reach, max(-(-total // amount), total * weights[0] // sum(weights)))
    least = 1 if total - largest >= amount - 1 else 0
    holding, spare = [largest] + [least] * (amount - 1), total - largest - least * (amount - 1)
    while spare > 0:
        movable = [i for i in range(1, amount) if holding[i] < largest] or [i for i in range(1, amount) if holding[i] < reach]
        whole, left = sum([weights[i] for i in movable]), spare
        for i in movable:
            more = min(reach - holding[i], max(1, left * weights[i] // whole), spare)
            holding[i] = holding[i] + more
            spare = spare - more
    return np.array(holding)


def noise(key, shape, deviation, reach, split=(), kind=jnp.bfloat16):
    array = jax.random.normal(key, shape, jnp.float32) * deviation
    if len(split) > 0:
        array = steps_of(key, shape, split, -0.22, 0.18) * array
    return jnp.clip(array, min=-reach, max=reach).astype(kind)


def setup_inputs(seed: int = 0) -> dict:
    splits = jax.random.split(jax.random.key(seed), 7)
    tokens = noise(splits[0], (TOKENS, D), 1.0, 6.0, ((0, 128),))
    expert_ids_keys = jax.random.split(jax.random.fold_in(splits[1], 1), TOKENS // TOK_DEV)
    expert_ids_turns = jax.random.permutation(jax.random.fold_in(splits[1], 3), TOKENS // TOK_DEV)
    expert_ids = jax.vmap(lambda own, number: assign_block(jax.random.fold_in(splits[1], 2), own, number, TOK_DEV, EXPERTS, TOP, CAP, 2))(expert_ids_keys, expert_ids_turns).reshape((TOKENS, TOP))
    gate_weights = jnp.clip(jnp.exp(math.log(0.5) - 2.3025851 * jax.random.uniform(splits[2], (TOKENS, TOP), jnp.float32) ** steps_of(splits[2], (TOKENS, TOP), ((0, 128),), -0.2, 0.2)), 0.05, 0.5)
    w_gate = noise(splits[3], (EXPERTS, D, H), D ** -0.5, 0.09375, ((0, 128),))
    w_up = noise(splits[4], (EXPERTS, D, H), D ** -0.5, 0.09375, ((0, 128),))
    w_down = noise(splits[5], (EXPERTS, H, D), H ** -0.5, 0.1875, ((0, 128),))
    return {"tokens": tokens, "expert_ids": expert_ids, "gate_weights": gate_weights, "w_gate": w_gate, "w_up": w_up, "w_down": w_down}


def reference(tokens, expert_ids, gate_weights, w_gate, w_up, w_down):
    flat_e = expert_ids.reshape(-1).astype(jnp.int32)
    flat_gate = gate_weights.reshape(-1)
    sort_order = jnp.argsort(flat_e, stable=True).astype(jnp.int32)
    sorted_e = flat_e[sort_order]
    labels = jnp.arange(EXPERTS, dtype=jnp.int32)
    starts = jnp.searchsorted(sorted_e, labels, side="left").astype(jnp.int32)
    finish = jnp.searchsorted(sorted_e, labels, side="right").astype(jnp.int32)
    row_limit = N_GROUP * N_LOCAL * CAP
    padded = jnp.concatenate([sort_order, jnp.zeros((row_limit,), jnp.int32)])

    def visit(accumulated, expert):
        picked = lax.dynamic_slice_in_dim(padded, starts[expert], row_limit)
        token_index = (picked // TOP).astype(jnp.int32)
        chosen = tokens[token_index]
        gate_part = jnp.dot(chosen, w_gate[expert], preferred_element_type=jnp.float32)
        lin_part = jnp.dot(chosen, w_up[expert], preferred_element_type=jnp.float32)
        hidden = (jax.nn.silu(gate_part) * lin_part).astype(jnp.bfloat16)
        output = jnp.dot(hidden, w_down[expert], preferred_element_type=jnp.float32).astype(jnp.bfloat16)
        live_mask = jnp.arange(row_limit, dtype=jnp.int32) < (finish[expert] - starts[expert])
        weights_now = jnp.where(live_mask, flat_gate[picked], jnp.zeros_like(flat_gate[picked]))
        term = weights_now[:, None] * output.astype(accumulated.dtype)
        return accumulated.at[token_index].add(term), None

    initial = jnp.zeros((tokens.shape[0], tokens.shape[1]), jnp.float32)
    total, unused = lax.scan(visit, initial, labels)
    return total.astype(jnp.bfloat16)
```

```python
import jax
import jax.numpy as jnp
from jax import lax
from jax.sharding import PartitionSpec as P

CAP = 10


def body(tokens, expert_ids, gate_weights, w_gate, w_up, w_down):
    rows, width = tokens.shape
    experts = lax.axis_size("group") * lax.axis_size("local")
    quarter = width // 4
    labels = jnp.arange(experts, dtype=jnp.int32)
    hit = expert_ids[:, :, None] == labels[None, None, :]
    named = jnp.any(hit, axis=1)
    weight_te = jnp.sum(jnp.where(hit, gate_weights[:, :, None], 0.0), axis=1)
    below = (jnp.arange(rows)[:, None] > jnp.arange(rows)[None, :]).astype(jnp.bfloat16)
    place = jnp.dot(below, named.astype(jnp.bfloat16), preferred_element_type=jnp.float32).astype(jnp.int32)
    place = jnp.where(named, place, -1)
    pick = place.T[:, None, :] == jnp.arange(CAP, dtype=jnp.int32)[None, :, None]
    pick_bf = pick.reshape(experts * CAP, rows).astype(jnp.bfloat16)
    parts = [
        jnp.dot(pick_bf, tokens[:, q * quarter:(q + 1) * quarter], preferred_element_type=jnp.bfloat16)
        .reshape(experts, CAP, quarter)
        for q in range(4)
    ]
    arrived = lax.all_to_all(jnp.concatenate(parts, axis=1), ("group", "local"), split_axis=0, concat_axis=0, tiled=True)
    flat = jnp.concatenate(
        [arrived[:, q * CAP:(q + 1) * CAP].reshape(experts * CAP, quarter) for q in range(4)], axis=1
    )
    gate_part = jnp.dot(flat, w_gate[0], preferred_element_type=jnp.float32)
    lin_part = jnp.dot(flat, w_up[0], preferred_element_type=jnp.float32)
    hidden = (jax.nn.silu(gate_part) * lin_part).astype(jnp.bfloat16)
    results = jnp.concatenate(
        [
            jnp.dot(hidden, w_down[0][:, q * quarter:(q + 1) * quarter], preferred_element_type=jnp.float32)
            .astype(jnp.bfloat16)
            .reshape(experts, CAP, quarter)
            for q in range(4)
        ],
        axis=1,
    )
    returned = lax.all_to_all(results, ("group", "local"), split_axis=0, concat_axis=0, tiled=True)
    spread = jnp.where(pick, weight_te.T[:, None, :], 0.0).reshape(experts * CAP, rows)
    high = spread.astype(jnp.bfloat16)
    low = (spread - high.astype(jnp.float32)).astype(jnp.bfloat16)
    both = jnp.concatenate([high, low], axis=1)
    out = []
    for q in range(4):
        back = returned[:, q * CAP:(q + 1) * CAP].reshape(experts * CAP, quarter)
        total = lax.dot_general(both, back, (((0,), (0,)), ((), ())), preferred_element_type=jnp.float32)
        out.append((total[:rows] + total[rows:]).astype(jnp.bfloat16))
    return jnp.concatenate(out, axis=1)


def solution(mesh):
    spec = P(("group", "local"), None)
    wide = P(("group", "local"), None, None)
    return jax.shard_map(
        body, mesh=mesh, in_specs=(spec, spec, spec, wide, wide, wide), out_specs=spec, check_vma=False
    )
```

```python
import functools

import jax
import jax.numpy as jnp
from jax import lax
from jax.experimental import pallas as pl
from jax.experimental.pallas import tpu as pltpu
from jax.sharding import PartitionSpec as P

CAP = 10
SIDE = 4
CORES = 2
BLOCK = SIDE * CAP
SLOTS = SIDE * CORES * BLOCK
LANES = 384
ORDERS = ((0, 1, 2), (1, 2, 0), (2, 0, 1))
WIDTHS = (1152, 1280, 1152)
STARTS = (0, 1152, 2432)
TILES = (384, 256, 384)
RING = (1, 3, 2)
BF16 = jnp.bfloat16
F32 = jnp.float32


def whereabouts():
    group, local = lax.axis_index("group"), lax.axis_index("local")
    return (group // SIDE, group % SIDE, local // CORES), local % CORES


def device_at(pos, core):
    return (pos[0] * SIDE + pos[1], pos[2] * CORES + core)


def along(pos, axis, value):
    return tuple(value if a == axis else pos[a] for a in range(3))


def greet(pos, core):
    barrier = pltpu.get_barrier_semaphore()
    peers = [device_at(pos, 1 - core)]
    for axis in range(3):
        for step in RING:
            for other in range(CORES):
                there = along(pos, axis, (pos[axis] + step) % SIDE)
                peers.append(device_at(there, (core + other) % CORES))
    for peer in peers:
        pl.semaphore_signal(barrier, inc=1, device_id=peer, device_id_type=pl.DeviceIdType.MESH)
    pl.semaphore_wait(barrier, len(peers))


def send(src, dst, send_sem, recv_sem, device):
    return pltpu.make_async_remote_copy(
        src_ref=src, dst_ref=dst, send_sem=send_sem, recv_sem=recv_sem,
        device_id=device, device_id_type=pl.DeviceIdType.MESH,
    )


LAST = tuple((step, other) for step in RING for other in range(CORES)) + ((0, 1),)


def dispatch_kernel(tok, meta, xa, xb, xc, mixed, ga, gb, gc, sa, sb, sc, ra, rb, rc, notes, picks,
                    s1, r1, sm, rm, s2, r2, s3, r3, keep):
    pos, core = whereabouts()
    outs, gathered, cut, relay = (xa, xb, xc), (ga, gb, gc), (sa, sb, sc), (ra, rb, rc)
    greet(pos, core)
    first = []
    for step in RING:
        for p, (a1, _, _) in enumerate(ORDERS):
            there = (pos[a1] + step) % SIDE
            peer = device_at(along(pos, a1, there), core)
            first.append(send(meta.at[p, there], notes.at[p, pos[a1]], sm.at[p, step], rm.at[p, pos[a1]], peer))
            first[-1].start()
            columns = pl.ds(STARTS[p], WIDTHS[p])
            first.append(send(tok.at[:, columns], gathered[p].at[pos[a1]], s1.at[p, step], r1.at[p, pos[a1]], peer))
            first[-1].start()
    for p, (a1, _, _) in enumerate(ORDERS):
        gathered[p][pos[a1]] = tok[:, STARTS[p]:STARTS[p] + WIDTHS[p]]
        notes[p, pos[a1]] = meta[p, pos[a1]]

    second, third, local = [], [], []

    def forward(p, step):
        a1, a2, a3 = ORDERS[p]
        origin = (pos[a2] + step) % SIDE
        source = cut[p] if step == 0 else relay[p]
        mine = pos[a3] * CORES + core
        for j, (way, other) in enumerate(LAST):
            there = (pos[a3] + way) % SIDE
            side = (core + other) % CORES
            third.append(send(
                source.at[origin, there * CORES + side], outs[p].at[mine, origin],
                s3.at[p, step, j], r3.at[p, origin, mine], device_at(along(pos, a3, there), side),
            ))
            third[-1].start()
        local.append(pltpu.make_async_copy(source.at[origin, mine], outs[p].at[mine, origin], keep.at[p, step]))
        local[-1].start()

    for p, (a1, a2, a3) in enumerate(ORDERS):
        for step in RING:
            there = (pos[a1] + step) % SIDE
            peer = device_at(along(pos, a1, there), core)
            send(meta.at[p, there], notes.at[p, there], sm.at[p, step], rm.at[p, there], peer).wait_recv()
            columns = pl.ds(STARTS[p], WIDTHS[p])
            send(tok.at[:, columns], gathered[p].at[there], s1.at[p, step], r1.at[p, there], peer).wait_recv()
        largest = jnp.maximum(jnp.maximum(notes[p, 0], notes[p, 1]), jnp.maximum(notes[p, 2], notes[p, 3]))
        total = notes[p, 0] + notes[p, 1] + notes[p, 2] + notes[p, 3]
        row = lax.broadcasted_iota(jnp.int32, (8, LANES), 0)
        table = jnp.where(row < SIDE, largest, total)
        mixed[p] = table
        turned = table.T
        place = lax.broadcasted_iota(jnp.int32, (SLOTS, SIDE * 128), 1).astype(F32)
        for there in range(SIDE):
            picks[there] = (turned[:SLOTS, there:there + 1] == place).astype(BF16)
        for step in RING + (0,):
            there = (pos[a2] + step) % SIDE

            @pl.loop(0, WIDTHS[p] // TILES[p])
            def _(n):
                columns = pl.ds(pl.multiple_of(n * TILES[p], 128), TILES[p])
                rows = gathered[p][:, :, columns].reshape(SIDE * 128, TILES[p])
                found = jnp.dot(picks[there], rows, preferred_element_type=F32)
                for d in range(SIDE * CORES):
                    cut[p][there, d, :, columns] = found[d * BLOCK:(d + 1) * BLOCK].astype(BF16)

            if step:
                second.append(send(
                    cut[p].at[there], relay[p].at[pos[a2]], s2.at[p, step], r2.at[p, pos[a2]],
                    device_at(along(pos, a2, there), core),
                ))
                second[-1].start()
            else:
                forward(p, 0)
    for step in (3, 1, 2):
        for p, (a1, a2, a3) in enumerate(ORDERS):
            there = (pos[a2] + step) % SIDE
            send(
                cut[p].at[there], relay[p].at[there], s2.at[p, step], r2.at[p, there],
                device_at(along(pos, a2, there), core),
            ).wait_recv()
            forward(p, step)
    for p, (a1, a2, a3) in enumerate(ORDERS):
        for step in range(SIDE):
            origin = (pos[a2] + step) % SIDE
            for j, (way, other) in enumerate(LAST):
                there = (pos[a3] + way) % SIDE
                side = (core + other) % CORES
                from_d = there * CORES + side
                send(
                    cut[p].at[origin, from_d], outs[p].at[from_d, origin],
                    s3.at[p, step, j], r3.at[p, origin, from_d], device_at(along(pos, a3, there), side),
                ).wait_recv()
    for copy in first + second + third:
        copy.wait_send()
    for copy in local:
        copy.wait()


def return_kernel(ya, yb, yc, mixed, out, la, lb, lc, ha, hb, hc, pa, pb, pc, qa, qb, qc, spread,
                  s3, r3, s2, r2, s1, r1, keep):
    pos, core = whereabouts()
    results, landed, home, parts, others = (ya, yb, yc), (la, lb, lc), (ha, hb, hc), (pa, pb, pc), (qa, qb, qc)
    greet(pos, core)
    sent, local = [], []
    for step in RING + (0,):
        for p, (a1, a2, a3) in enumerate(ORDERS):
            owner = (pos[a2] + step) % SIDE
            mine = pos[a3] * CORES + core
            for j, (way, other) in enumerate(LAST):
                there = (pos[a3] + way) % SIDE
                side = (core + other) % CORES
                sent.append(send(
                    results[p].at[there * CORES + side, owner], landed[p].at[owner, mine],
                    s3.at[p, step, j], r3.at[p, owner, mine], device_at(along(pos, a3, there), side),
                ))
                sent[-1].start()
            local.append(pltpu.make_async_copy(
                results[p].at[mine, owner], landed[p].at[owner, mine], keep.at[p, step]
            ))
            local[-1].start()
    local_at = 0
    for step in RING + (0,):
        for p, (a1, a2, a3) in enumerate(ORDERS):
            owner = (pos[a2] + step) % SIDE
            for j, (way, other) in enumerate(LAST):
                there = (pos[a3] + way) % SIDE
                side = (core + other) % CORES
                from_d = there * CORES + side
                send(
                    results[p].at[from_d, owner], landed[p].at[owner, from_d],
                    s3.at[p, step, j], r3.at[p, owner, from_d], device_at(along(pos, a3, there), side),
                ).wait_recv()
            local[local_at].wait()
            local_at += 1
            if step:
                sent.append(send(
                    landed[p].at[owner], home[p].at[pos[a2]], s2.at[p, step], r2.at[p, pos[a2]],
                    device_at(along(pos, a2, owner), core),
                ))
                sent[-1].start()
    for p, (a1, a2, a3) in enumerate(ORDERS):
        token = lax.broadcasted_iota(jnp.int32, (SIDE * 128, SLOTS), 0).astype(F32)
        for there in range(SIDE):
            index = mixed[p, there:there + 1, :SLOTS]
            weight = mixed[p, SIDE + there:SIDE + there + 1, :SLOTS]
            spread[there] = jnp.where(token == index, weight, 0.0).astype(BF16)
        for step in RING:
            there = (pos[a2] + step) % SIDE
            send(
                landed[p].at[there], home[p].at[there], s2.at[p, step], r2.at[p, there],
                device_at(along(pos, a2, there), core),
            ).wait_recv()

        @pl.loop(0, WIDTHS[p] // TILES[p])
        def _(n):
            columns = pl.ds(pl.multiple_of(n * TILES[p], 128), TILES[p])
            total = jnp.zeros((SIDE * 128, TILES[p]), F32)
            for step in range(SIDE):
                there = (pos[a2] + step) % SIDE
                source = home[p] if step else landed[p]
                rows = source[there, :, :, columns].astype(F32).reshape(SLOTS, TILES[p]).astype(BF16)
                total = total + jnp.dot(spread[there], rows, preferred_element_type=F32)
            for k in range(SIDE):
                parts[p][k, :, columns] = total[k * 128:(k + 1) * 128].astype(BF16)

        for step in RING:
            there = (pos[a1] + step) % SIDE
            sent.append(send(
                parts[p].at[there], others[p].at[pos[a1]], s1.at[p, step], r1.at[p, pos[a1]],
                device_at(along(pos, a1, there), core),
            ))
            sent[-1].start()
    for p, (a1, a2, a3) in enumerate(ORDERS):
        total = parts[p][pos[a1]].astype(F32)
        for step in RING:
            there = (pos[a1] + step) % SIDE
            send(
                parts[p].at[there], others[p].at[there], s1.at[p, step], r1.at[p, there],
                device_at(along(pos, a1, there), core),
            ).wait_recv()
            total = total + others[p][there].astype(F32)
        out[:, STARTS[p]:STARTS[p] + WIDTHS[p]] = total.astype(BF16)
    for copy in sent:
        copy.wait_send()


def expert_kernel(xa, xb, xc, wg, wu, wd, turn, ya, yb, yc, va, vb, vc, gate_w, up_w, down_w, turns, full, hid, hid_a, hid_c,
                  xsem, wsem, ysem):
    arrived, held, results = (xa, xb, xc), (va, vb, vc), (ya, yb, yc)
    loads = [pltpu.make_async_copy(turn, turns, wsem.at[3])]
    loads += [pltpu.make_async_copy(arrived[p], held[p], xsem.at[p]) for p in range(3)]
    weights = [pltpu.make_async_copy(a, b, wsem.at[i]) for i, (a, b) in enumerate(((wg, gate_w), (wu, up_w), (wd, down_w)))]
    for copy in loads + weights:
        copy.start()
    for copy in loads:
        copy.wait()
    stores = []
    for side in range(CORES):
        for p in range(3):
            @pl.loop(0, WIDTHS[p] // TILES[p])
            def _(n):
                columns = pl.ds(pl.multiple_of(n * TILES[p], 128), TILES[p])
                rows = held[p][:, side, :, columns].reshape(SIDE * SIDE * BLOCK, TILES[p])
                if p != 1:
                    rows = jnp.dot(turns[p // 2], rows, preferred_element_type=F32).astype(BF16)
                full[:, pl.ds(pl.multiple_of(STARTS[p] + n * TILES[p], 128), TILES[p])] = rows
        if side == 0:
            weights[0].wait()
            weights[1].wait()

        @pl.loop(0, 4)
        def _(n):
            columns = pl.ds(pl.multiple_of(n * 256, 128), 256)
            gate = jnp.dot(full[...], gate_w[:, columns], preferred_element_type=F32)
            lin = jnp.dot(full[...], up_w[:, columns], preferred_element_type=F32)
            hid[:, columns] = (gate * (1.0 / (1.0 + jnp.exp(-gate))) * lin).astype(BF16)

        @pl.loop(0, 4)
        def _(n):
            columns = pl.ds(pl.multiple_of(n * 256, 128), 256)
            hid_a[:, columns] = jnp.dot(turns[1], hid[:, columns], preferred_element_type=F32).astype(BF16)
            hid_c[:, columns] = jnp.dot(turns[0], hid[:, columns], preferred_element_type=F32).astype(BF16)

        if side == 0:
            weights[2].wait()
        for p, rows in enumerate((hid_a, hid, hid_c)):
            @pl.loop(0, WIDTHS[p] // TILES[p])
            def _(n):
                columns = pl.ds(pl.multiple_of(n * TILES[p], 128), TILES[p])
                of_w = pl.ds(pl.multiple_of(STARTS[p] + n * TILES[p], 128), TILES[p])
                result = jnp.dot(rows[...], down_w[:, of_w], preferred_element_type=F32).astype(BF16)
                held[p][:, side, :, columns] = result.reshape(SIDE, SIDE * BLOCK, TILES[p])

            stores.append(pltpu.make_async_copy(held[p].at[:, side], results[p].at[:, side], ysem.at[p, side]))
            stores[-1].start()
    for copy in stores:
        copy.wait()


ANY = pl.BlockSpec(memory_space=pl.ANY)
VMEM = pl.BlockSpec(memory_space=pltpu.VMEM)
DMA = pltpu.SemaphoreType.DMA


def blocks(leading):
    return [jax.ShapeDtypeStruct(leading + (w,), BF16) for w in WIDTHS]


def scratch(leading):
    return [pltpu.VMEM(leading + (w,), BF16) for w in WIDTHS]


def turn_matrices():
    row = jnp.arange(SIDE * SIDE * BLOCK, dtype=jnp.int32)
    k, i, j, s = row // 160, row // 40 % 4, row // 10 % 4, row % 10
    there = (i * 160 + j * 40 + k * 10 + s)[:, None] == row[None, :]
    return jnp.stack([there, there.T]).astype(BF16)


def tables(expert_ids, gate_weights):
    rows = expert_ids.shape[0]
    experts = SIDE ** 3 * CORES
    hit = expert_ids[:, :, None] == jnp.arange(experts, dtype=jnp.int32)[None, None, :]
    named = jnp.any(hit, axis=1)
    weight = jnp.sum(jnp.where(hit, gate_weights[:, :, None], 0.0), axis=1)
    below = (jnp.arange(rows)[:, None] > jnp.arange(rows)[None, :]).astype(BF16)
    place = jnp.dot(below, named.astype(BF16), preferred_element_type=F32).astype(jnp.int32)
    place = jnp.where(named, place, -1)
    pick = place.T[:, None, :] == jnp.arange(CAP, dtype=jnp.int32)[None, :, None]
    token = jnp.max(jnp.where(pick, jnp.arange(rows, dtype=jnp.int32).astype(F32)[None, None, :], -1.0), axis=2)
    amount = jnp.sum(jnp.where(pick, weight.T[:, None, :], 0.0), axis=2)
    shape = (SIDE, SIDE, SIDE, CORES, CAP)
    token, amount = token.reshape(shape), amount.reshape(shape)
    pos, _ = whereabouts()
    made = []
    for a1, a2, a3 in ORDERS:
        mine = (jnp.arange(SIDE) == pos[a1])[None, None, None, None, :, None]
        order = (a1, a2, a3, 3, 4)
        index = token.transpose(order)[:, :, :, :, None, :]
        index = jnp.where(mine & (index >= 0), index + (128 * pos[a1]).astype(F32), -1.0)
        value = jnp.where(mine, amount.transpose(order)[:, :, :, :, None, :], 0.0)
        index = jnp.pad(index.reshape(SIDE, SIDE, SLOTS), ((0, 0), (0, 0), (0, LANES - SLOTS)), constant_values=-1.0)
        value = jnp.pad(value.reshape(SIDE, SIDE, SLOTS), ((0, 0), (0, 0), (0, LANES - SLOTS)))
        made.append(jnp.concatenate([index, value], axis=1))
    return jnp.stack(made)


def body(tokens, expert_ids, gate_weights, w_gate, w_up, w_down):
    meta = tables(expert_ids, gate_weights)
    params = functools.partial(pltpu.CompilerParams, vmem_limit_bytes=60 * 2 ** 20)
    D8 = SIDE * CORES
    *arrived, mixed = pl.pallas_call(
        dispatch_kernel,
        out_shape=blocks((D8, SIDE, BLOCK)) + [jax.ShapeDtypeStruct((3, 8, LANES), F32)],
        in_specs=[VMEM, VMEM],
        out_specs=[ANY, ANY, ANY, VMEM],
        scratch_shapes=scratch((SIDE, 128)) + scratch((SIDE, D8, BLOCK)) + scratch((SIDE, D8, BLOCK)) + [
            pltpu.VMEM((3, SIDE, 8, LANES), F32),
            pltpu.VMEM((SIDE, SLOTS, SIDE * 128), BF16),
        ] + [DMA((3, SIDE))] * 6 + [DMA((3, SIDE, 7)), DMA((3, SIDE, D8)), DMA((3, SIDE))],
        compiler_params=params(collective_id=0, has_side_effects=True),
        name="dispatch",
    )(tokens, meta)
    arrived = [a.reshape(SIDE, CORES, SIDE * BLOCK, a.shape[-1]) for a in arrived]
    half = SIDE * SIDE * BLOCK
    results = pl.pallas_call(
        expert_kernel,
        out_shape=blocks((SIDE, CORES, SIDE * BLOCK)),
        in_specs=[ANY] * 7,
        out_specs=[ANY] * 3,
        scratch_shapes=scratch((SIDE, CORES, SIDE * BLOCK)) + [
            pltpu.VMEM(w_gate.shape[1:], BF16), pltpu.VMEM(w_up.shape[1:], BF16), pltpu.VMEM(w_down.shape[1:], BF16),
            pltpu.VMEM((2, half, half), BF16),
            pltpu.VMEM((half, tokens.shape[1]), BF16),
        ] + [pltpu.VMEM((half, w_gate.shape[2]), BF16)] * 3 + [DMA((3,)), DMA((4,)), DMA((3, CORES))],
        compiler_params=params(),
        name="expert",
    )(*arrived, w_gate[0], w_up[0], w_down[0], turn_matrices())
    results = [r.reshape(D8, SIDE, BLOCK, r.shape[-1]) for r in results]
    return pl.pallas_call(
        return_kernel,
        out_shape=jax.ShapeDtypeStruct(tokens.shape, BF16),
        in_specs=[ANY] * 3 + [VMEM],
        out_specs=VMEM,
        scratch_shapes=scratch((SIDE, D8, BLOCK)) + scratch((SIDE, D8, BLOCK)) + scratch((SIDE, 128)) + scratch((SIDE, 128)) + [
            pltpu.VMEM((SIDE, SIDE * 128, SLOTS), BF16),
        ] + [DMA((3, SIDE, 7)), DMA((3, SIDE, D8))] + [DMA((3, SIDE))] * 5,
        compiler_params=params(collective_id=1, has_side_effects=True),
        name="give_back",
    )(*results, mixed)


def solution(mesh):
    spec = P(("group", "local"), None)
    wide = P(("group", "local"), None, None)
    return jax.shard_map(
        body, mesh=mesh, in_specs=(spec, spec, spec, wide, wide, wide), out_specs=spec, check_vma=False
    )
```

```python
import jax
import jax.numpy as jnp
from jax import lax
from jax.experimental import pallas as pl
from jax.experimental.pallas import tpu as pltpu
from jax.sharding import PartitionSpec as P

CAP = 10
SIDE = 4
CORES = 2
BLOCK = SIDE * CAP
SLOTS = SIDE * CORES * BLOCK
HALF = SIDE * SIDE * BLOCK
LANES = 384
ORDERS = ((0, 1, 2), (1, 2, 0), (2, 0, 1))
WIDTHS = (1152, 1280, 1152)
STARTS = (0, 1152, 2432)
TILES = (384, 256, 384)
RING = (1, 3, 2)
BF16 = jnp.bfloat16
F32 = jnp.float32


def whereabouts():
    group, local = lax.axis_index("group"), lax.axis_index("local")
    return (group // SIDE, group % SIDE, local // CORES), local % CORES


def device_at(pos, core):
    return (pos[0] * SIDE + pos[1], pos[2] * CORES + core)


def along(pos, axis, value):
    return tuple(value if a == axis else pos[a] for a in range(3))


def greet(pos, core):
    barrier = pltpu.get_barrier_semaphore()
    peers = [device_at(pos, 1 - core)]
    for axis in range(3):
        for step in RING:
            for other in range(CORES):
                there = along(pos, axis, (pos[axis] + step) % SIDE)
                peers.append(device_at(there, (core + other) % CORES))
    for peer in peers:
        pl.semaphore_signal(barrier, inc=1, device_id=peer, device_id_type=pl.DeviceIdType.MESH)
    pl.semaphore_wait(barrier, len(peers))


def send(src, dst, send_sem, recv_sem, device):
    return pltpu.make_async_remote_copy(
        src_ref=src, dst_ref=dst, send_sem=send_sem, recv_sem=recv_sem,
        device_id=device, device_id_type=pl.DeviceIdType.MESH,
    )


def layer_kernel(tok, meta, wg, wu, wd, turn, out, ra, rb, rc, la, lb, lc, ha, hb, hc,
                 ga, gb, gc, sa, sb, sc, xa, xb, xc, qa, qb, qc, gate_w, up_w, down_w, turns, full, hid, hid_t, notes, mixed,
                 wsem, s1, r1, sm, rm, s2, r2, s3, r3, keep, t3, u3, keep_t, t2, u2, fetch, t1, u1):
    pos, core = whereabouts()
    gathered, cut, relay, held = (ga, gb, gc), (sa, sb, sc), (ra, rb, rc), (xa, xb, xc)
    landed, home, others = (la, lb, lc), (ha, hb, hc), (qa, qb, qc)
    loads = [
        pltpu.make_async_copy(a, b, wsem.at[i])
        for i, (a, b) in enumerate(((turn, turns), (wg, gate_w), (wu, up_w), (wd, down_w)))
    ]
    for copy in loads:
        copy.start()
    greet(pos, core)

    def spot(p, stage, step):
        return (pos[ORDERS[p][stage]] + step) % SIDE

    def mine(p, stage):
        return pos[ORDERS[p][stage]]

    def peer(p, stage, step, other=0):
        return device_at(along(pos, ORDERS[p][stage], spot(p, stage, step)), (core + other) % CORES)

    def columns_of(p):
        return pl.ds(STARTS[p], WIDTHS[p])

    def tile(p, n, start=0):
        return pl.ds(pl.multiple_of(start + n * TILES[p], 128), TILES[p])

    def tables_out(p, step, slot):
        return send(meta.at[p, spot(p, 0, step)], notes.at[p, slot], sm.at[p, step], rm.at[p, slot], peer(p, 0, step))

    def tokens_out(p, step, slot):
        return send(
            tok.at[:, columns_of(p)], gathered[p].at[slot], s1.at[p, step], r1.at[p, slot], peer(p, 0, step)
        )

    def picked_out(p, step, h, slot):
        return send(
            cut[p].at[spot(p, 1, step), h], relay[p].at[slot, h], s2.at[p, step, h], r2.at[p, slot, h], peer(p, 1, step)
        )

    def block_source(p, step):
        return cut[p] if step == 0 else relay[p]

    def block_out(p, step, h, way, slot):
        origin = spot(p, 1, step)
        return send(
            block_source(p, step).at[origin, h, spot(p, 2, way)], held[p].at[h, slot, origin],
            s3.at[p, step, h, way], r3.at[p, origin, h, slot], peer(p, 2, way, h),
        )

    def block_kept(p, step):
        origin = spot(p, 1, step)
        return pltpu.make_async_copy(
            block_source(p, step).at[origin, 0, mine(p, 2)], held[p].at[0, mine(p, 2), origin], keep.at[p, step]
        )

    def result_out(p, step, h, way, slot):
        owner = spot(p, 1, step)
        return send(
            held[p].at[h, spot(p, 2, way), owner], landed[p].at[owner, h, slot],
            t3.at[p, step, h, way], u3.at[p, owner, h, slot], peer(p, 2, way, h),
        )

    def result_kept(p, step):
        owner = spot(p, 1, step)
        return pltpu.make_async_copy(
            held[p].at[0, mine(p, 2), owner], landed[p].at[owner, 0, mine(p, 2)], keep_t.at[p, step]
        )

    def result_on(p, step, h, slot):
        return send(
            landed[p].at[spot(p, 1, step), h], home[p].at[slot, h], t2.at[p, step, h], u2.at[p, slot, h], peer(p, 1, step)
        )

    def fetched(p, step, h):
        origin = spot(p, 1, step)
        source = home[p] if step else landed[p]
        return pltpu.make_async_copy(source.at[origin, h], cut[p].at[origin, h], fetch.at[p, step, h])

    def sum_out(p, step, slot):
        return send(
            gathered[p].at[spot(p, 0, step)], others[p].at[slot], t1.at[p, step], u1.at[p, slot], peer(p, 0, step)
        )

    def ways(h):
        return RING + (0,) * h

    def forward(p, step, h):
        for way in ways(h):
            block_out(p, step, h, way, mine(p, 2)).start()
        if h == 0:
            block_kept(p, step).start()

    with jax.named_scope("send_tokens"):
        for step in RING:
            for p in range(3):
                tables_out(p, step, mine(p, 0)).start()
                tokens_out(p, step, mine(p, 0)).start()
        for p in range(3):
            gathered[p][mine(p, 0)] = tok[:, STARTS[p]:STARTS[p] + WIDTHS[p]]
            notes[p, mine(p, 0)] = meta[p, mine(p, 0)]

    with jax.named_scope("pick_rows"):
        for p in range(3):
            for step in RING:
                tables_out(p, step, spot(p, 0, step)).wait_recv()
                tokens_out(p, step, spot(p, 0, step)).wait_recv()
            largest = jnp.maximum(jnp.maximum(notes[p, 0], notes[p, 1]), jnp.maximum(notes[p, 2], notes[p, 3]))
            total = notes[p, 0] + notes[p, 1] + notes[p, 2] + notes[p, 3]
            table = jnp.where(lax.broadcasted_iota(jnp.int32, (8, LANES), 0) < SIDE, largest, total)
            mixed[p] = table
            turned = table.T
            place = lax.broadcasted_iota(jnp.int32, (SLOTS, SIDE * 128), 1).astype(F32)
            for there in range(SIDE):
                full[:SLOTS, there * 512:(there + 1) * 512] = (turned[:SLOTS, there:there + 1] == place).astype(BF16)
            for step in RING + (0,):
                there = spot(p, 1, step)
                picks = pl.ds(pl.multiple_of(there * 512, 512), 512)

                @pl.loop(0, WIDTHS[p] // TILES[p])
                def _(n):
                    rows = gathered[p][:, :, tile(p, n)].reshape(SIDE * 128, TILES[p])
                    found = jnp.dot(full[:SLOTS, picks], rows, preferred_element_type=F32)
                    for d in range(SIDE * CORES):
                        cut[p][there, d // SIDE, d % SIDE, :, tile(p, n)] = found[d * BLOCK:(d + 1) * BLOCK].astype(BF16)

                if step:
                    picked_out(p, step, 0, mine(p, 1)).start()
                else:
                    forward(p, 0, 0)
    with jax.named_scope("second_half"):
        for step in RING:
            for p in range(3):
                picked_out(p, step, 1, mine(p, 1)).start()
        for p in range(3):
            forward(p, 0, 1)

    with jax.named_scope("relay_rows"):
        for h in range(CORES):
            for step in (3, 1, 2):
                for p in range(3):
                    picked_out(p, step, h, spot(p, 1, step)).wait_recv()
                    forward(p, step, h)

    def arrive(h):
        for p in range(3):
            for step in range(SIDE):
                for way in ways(h):
                    block_out(p, step, h, way, spot(p, 2, way)).wait_recv()
                if h == 0:
                    block_kept(p, step).wait()

    def line_up(h):
        for p in range(3):
            @pl.loop(0, WIDTHS[p] // TILES[p])
            def _(n):
                rows = held[p][h, :, :, :, tile(p, n)].astype(F32).reshape(HALF, TILES[p]).astype(BF16)
                if p != 1:
                    rows = jnp.dot(turns[p // 2], rows, preferred_element_type=F32).astype(BF16)
                full[:, tile(p, n, STARTS[p])] = rows

    def hide():
        @pl.loop(0, 4)
        def _(n):
            columns = pl.ds(pl.multiple_of(n * 256, 128), 256)
            gate = jnp.dot(full[...], gate_w[:, columns], preferred_element_type=F32)
            lin = jnp.dot(full[...], up_w[:, columns], preferred_element_type=F32)
            hid[:, columns] = (gate * (1.0 / (1.0 + jnp.exp(-gate))) * lin).astype(BF16)

    def answer(h, p):
        rows = hid if p == 1 else hid_t
        if p != 1:
            @pl.loop(0, 4)
            def _(n):
                columns = pl.ds(pl.multiple_of(n * 256, 128), 256)
                hid_t[:, columns] = jnp.dot(turns[1 - p // 2], hid[:, columns], preferred_element_type=F32).astype(BF16)

        @pl.loop(0, WIDTHS[p] // TILES[p])
        def _(n):
            result = jnp.dot(rows[...], down_w[:, tile(p, n, STARTS[p])], preferred_element_type=F32)
            for b in range(SIDE * SIDE):
                block = result[b * BLOCK:(b + 1) * BLOCK].astype(BF16)
                held[p][h, b // SIDE, b % SIDE, :, tile(p, n)] = block

        for step in RING + (0,):
            for way in ways(h):
                result_out(p, step, h, way, mine(p, 2)).start()
            if h == 0:
                result_kept(p, step).start()

    def landing(p, step, h):
        for way in ways(h):
            result_out(p, step, h, way, spot(p, 2, way)).wait_recv()
        if h == 0:
            result_kept(p, step).wait()

    with jax.named_scope("arrive_own"):
        arrive(0)
    with jax.named_scope("line_up"):
        loads[0].wait()
        line_up(0)
    with jax.named_scope("hidden"):
        loads[1].wait()
        loads[2].wait()
        hide()
    with jax.named_scope("answer"):
        loads[3].wait()
        for p in range(3):
            answer(0, p)
    with jax.named_scope("arrive_other"):
        arrive(1)
    with jax.named_scope("line_up"):
        line_up(1)
    with jax.named_scope("hidden"):
        hide()
    with jax.named_scope("relay_results_own"):
        for step in RING:
            for p in range(3):
                landing(p, step, 0)
                result_on(p, step, 0, mine(p, 1)).start()
    with jax.named_scope("answer"):
        for p in range(3):
            answer(1, p)
    with jax.named_scope("wait_sent"):
        for p in range(3):
            for step in RING:
                tables_out(p, step, mine(p, 0)).wait_send()
                tokens_out(p, step, mine(p, 0)).wait_send()
                for h in range(CORES):
                    picked_out(p, step, h, mine(p, 1)).wait_send()
            for step in range(SIDE):
                for h in range(CORES):
                    for way in ways(h):
                        block_out(p, step, h, way, mine(p, 2)).wait_send()
    with jax.named_scope("fetch_own"):
        for p in range(3):
            landing(p, 0, 0)
            fetched(p, 0, 0).start()
        for step in (3, 1, 2):
            for p in range(3):
                result_on(p, step, 0, spot(p, 1, step)).wait_recv()
                fetched(p, step, 0).start()
    with jax.named_scope("relay_results_other"):
        for step in RING:
            for p in range(3):
                landing(p, step, 1)
                result_on(p, step, 1, mine(p, 1)).start()
        for p in range(3):
            landing(p, 0, 1)
            fetched(p, 0, 1).start()

    with jax.named_scope("weighted_sum"):
        for p in range(3):
            token = lax.broadcasted_iota(jnp.int32, (SIDE * 128, SLOTS), 0).astype(F32)
            for there in range(SIDE):
                index = mixed[p, there:there + 1, :SLOTS]
                weight = mixed[p, SIDE + there:SIDE + there + 1, :SLOTS]
                full[:SIDE * 128, there * LANES:there * LANES + SLOTS] = jnp.where(token == index, weight, 0.0).astype(BF16)
            for step in (3, 1, 2):
                result_on(p, step, 1, spot(p, 1, step)).wait_recv()
                fetched(p, step, 1).start()
            for step in range(SIDE):
                for h in range(CORES):
                    fetched(p, step, h).wait()

            @pl.loop(0, WIDTHS[p] // TILES[p])
            def _(n):
                total = jnp.zeros((SIDE * 128, TILES[p]), F32)
                for there in range(SIDE):
                    rows = cut[p][there, :, :, :, tile(p, n)].astype(F32).reshape(SLOTS, TILES[p]).astype(BF16)
                    spread = full[:SIDE * 128, there * LANES:there * LANES + SLOTS]
                    total = total + jnp.dot(spread, rows, preferred_element_type=F32)
                for k in range(SIDE):
                    gathered[p][k, :, tile(p, n)] = total[k * 128:(k + 1) * 128].astype(BF16)

            for step in RING:
                sum_out(p, step, mine(p, 0)).start()
    with jax.named_scope("last_sum"):
        for p in range(3):
            total = gathered[p][mine(p, 0)].astype(F32)
            for step in RING:
                sum_out(p, step, spot(p, 0, step)).wait_recv()
                total = total + others[p][spot(p, 0, step)].astype(F32)
            out[:, STARTS[p]:STARTS[p] + WIDTHS[p]] = total.astype(BF16)
    for p in range(3):
        for step in RING:
            sum_out(p, step, mine(p, 0)).wait_send()
            for h in range(CORES):
                result_on(p, step, h, mine(p, 1)).wait_send()
        for step in range(SIDE):
            for h in range(CORES):
                for way in ways(h):
                    result_out(p, step, h, way, mine(p, 2)).wait_send()


ANY = pl.BlockSpec(memory_space=pl.ANY)
VMEM = pl.BlockSpec(memory_space=pltpu.VMEM)
DMA = pltpu.SemaphoreType.DMA


def blocks(leading):
    return [jax.ShapeDtypeStruct(leading + (w,), BF16) for w in WIDTHS]


def scratch(leading):
    return [pltpu.VMEM(leading + (w,), BF16) for w in WIDTHS]


def turn_matrices():
    row = jnp.arange(HALF, dtype=jnp.int32)
    k, i, j, s = row // 160, row // 40 % 4, row // 10 % 4, row % 10
    there = (i * 160 + j * 40 + k * 10 + s)[:, None] == row[None, :]
    return jnp.stack([there, there.T]).astype(BF16)


def tables(expert_ids, gate_weights):
    rows = expert_ids.shape[0]
    experts = SIDE ** 3 * CORES
    hit = expert_ids[:, :, None] == jnp.arange(experts, dtype=jnp.int32)[None, None, :]
    named = jnp.any(hit, axis=1)
    weight = jnp.sum(jnp.where(hit, gate_weights[:, :, None], 0.0), axis=1)
    below = (jnp.arange(rows)[:, None] > jnp.arange(rows)[None, :]).astype(BF16)
    place = jnp.dot(below, named.astype(BF16), preferred_element_type=F32).astype(jnp.int32)
    place = jnp.where(named, place, -1)
    pick = place.T[:, None, :] == jnp.arange(CAP, dtype=jnp.int32)[None, :, None]
    token = jnp.max(jnp.where(pick, jnp.arange(rows, dtype=jnp.int32).astype(F32)[None, None, :], -1.0), axis=2)
    amount = jnp.sum(jnp.where(pick, weight.T[:, None, :], 0.0), axis=2)
    shape = (SIDE, SIDE, SIDE, CORES, CAP)
    token, amount = token.reshape(shape), amount.reshape(shape)
    pos, core = whereabouts()
    token = jnp.where(core == 0, token, token[:, :, :, ::-1])
    amount = jnp.where(core == 0, amount, amount[:, :, :, ::-1])
    made = []
    for a1, a2, a3 in ORDERS:
        mine = (jnp.arange(SIDE) == pos[a1])[None, None, None, None, :, None]
        order = (a1, a2, 3, a3, 4)
        index = token.transpose(order)[:, :, :, :, None, :]
        index = jnp.where(mine & (index >= 0), index + (128 * pos[a1]).astype(F32), -1.0)
        value = jnp.where(mine, amount.transpose(order)[:, :, :, :, None, :], 0.0)
        index = jnp.pad(index.reshape(SIDE, SIDE, SLOTS), ((0, 0), (0, 0), (0, LANES - SLOTS)), constant_values=-1.0)
        value = jnp.pad(value.reshape(SIDE, SIDE, SLOTS), ((0, 0), (0, 0), (0, LANES - SLOTS)))
        made.append(jnp.concatenate([index, value], axis=1))
    return jnp.stack(made)


def body(tokens, expert_ids, gate_weights, w_gate, w_up, w_down):
    meta = tables(expert_ids, gate_weights)
    split = (SIDE, CORES, SIDE, BLOCK)
    out, *_ = pl.pallas_call(
        layer_kernel,
        out_shape=[jax.ShapeDtypeStruct(tokens.shape, BF16)] + blocks(split) * 3,
        in_specs=[VMEM, VMEM] + [ANY] * 4,
        out_specs=[VMEM] + [ANY] * 9,
        scratch_shapes=scratch((SIDE, 128)) + scratch(split) + scratch((CORES, SIDE, SIDE, BLOCK)) + scratch((SIDE, 128)) + [
            pltpu.VMEM(w_gate.shape[1:], BF16), pltpu.VMEM(w_up.shape[1:], BF16), pltpu.VMEM(w_down.shape[1:], BF16),
            pltpu.VMEM((2, HALF, HALF), BF16),
            pltpu.VMEM((HALF, tokens.shape[1]), BF16),
            pltpu.VMEM((HALF, w_gate.shape[2]), BF16),
            pltpu.VMEM((HALF, w_gate.shape[2]), BF16),
            pltpu.VMEM((3, SIDE, 8, LANES), F32),
            pltpu.VMEM((3, 8, LANES), F32),
        ] + [
            DMA((4,)), DMA((3, SIDE)), DMA((3, SIDE)), DMA((3, SIDE)), DMA((3, SIDE)),
            DMA((3, SIDE, CORES)), DMA((3, SIDE, CORES)), DMA((3, SIDE, CORES, SIDE)), DMA((3, SIDE, CORES, SIDE)),
            DMA((3, SIDE)), DMA((3, SIDE, CORES, SIDE)), DMA((3, SIDE, CORES, SIDE)), DMA((3, SIDE)),
            DMA((3, SIDE, CORES)), DMA((3, SIDE, CORES)), DMA((3, SIDE, CORES)), DMA((3, SIDE)), DMA((3, SIDE)),
        ],
        compiler_params=pltpu.CompilerParams(
            collective_id=0, has_side_effects=True, vmem_limit_bytes=62 * 2 ** 20
        ),
        name="layer",
    )(tokens, meta, w_gate[0], w_up[0], w_down[0], turn_matrices())
    return out


def solution(mesh):
    spec = P(("group", "local"), None)
    wide = P(("group", "local"), None, None)
    return jax.shard_map(
        body, mesh=mesh, in_specs=(spec, spec, spec, wide, wide, wide), out_specs=spec, check_vma=False
    )
```

```python
import jax
import jax.numpy as jnp
from jax import lax
from jax.experimental import pallas as pl
from jax.experimental.pallas import tpu as pltpu
from jax.sharding import PartitionSpec as P

CAP = 10
SIDE = 4
CORES = 2
BLOCK = SIDE * CAP
SLOTS = SIDE * CORES * BLOCK
HALF = SIDE * SIDE * BLOCK
LANES = 384
ORDERS = ((0, 1, 2), (1, 2, 0), (2, 0, 1))
WIDTHS = (1152, 1280, 1152)
STARTS = (0, 1152, 2432)
TILES = (384, 256, 384)
RING = (1, 3, 2)
BF16 = jnp.bfloat16
F32 = jnp.float32


def whereabouts():
    group, local = lax.axis_index("group"), lax.axis_index("local")
    return (group // SIDE, group % SIDE, local // CORES), local % CORES


def device_at(pos, core):
    return (pos[0] * SIDE + pos[1], pos[2] * CORES + core)


def along(pos, axis, value):
    return tuple(value if a == axis else pos[a] for a in range(3))


def greet(pos, core):
    barrier = pltpu.get_barrier_semaphore()
    peers = [device_at(pos, 1 - core)]
    for axis in range(3):
        for step in RING:
            for other in range(CORES):
                there = along(pos, axis, (pos[axis] + step) % SIDE)
                peers.append(device_at(there, (core + other) % CORES))
    for peer in peers:
        pl.semaphore_signal(barrier, inc=1, device_id=peer, device_id_type=pl.DeviceIdType.MESH)
    pl.semaphore_wait(barrier, len(peers))


def send(src, dst, send_sem, recv_sem, device):
    return pltpu.make_async_remote_copy(
        src_ref=src, dst_ref=dst, send_sem=send_sem, recv_sem=recv_sem,
        device_id=device, device_id_type=pl.DeviceIdType.MESH,
    )


def layer_kernel(tok, meta, wg, wu, wd, turn, out, ra, rb, rc, la, lb, lc, ha, hb, hc,
                 ga, gb, gc, sa, sb, sc, xa, xb, xc, qa, qb, qc, gate_w, up_w, down_w, turns, full, hid, hid_t, notes, mixed,
                 wsem, s1, r1, sm, rm, s2, r2, s3, r3, keep, t3, u3, keep_t, t2, u2, fetch, t1, u1):
    pos, core = whereabouts()
    gathered, cut, relay, held = (ga, gb, gc), (sa, sb, sc), (ra, rb, rc), (xa, xb, xc)
    landed, home, others = (la, lb, lc), (ha, hb, hc), (qa, qb, qc)
    loads = [
        pltpu.make_async_copy(a, b, wsem.at[i])
        for i, (a, b) in enumerate(((turn, turns), (wg, gate_w), (wu, up_w), (wd, down_w)))
    ]
    for copy in loads:
        copy.start()
    greet(pos, core)

    def spot(p, stage, step):
        return (pos[ORDERS[p][stage]] + step) % SIDE

    def mine(p, stage):
        return pos[ORDERS[p][stage]]

    def peer(p, stage, step, other=0):
        return device_at(along(pos, ORDERS[p][stage], spot(p, stage, step)), (core + other) % CORES)

    def columns_of(p):
        return pl.ds(STARTS[p], WIDTHS[p])

    def tile(p, n, start=0):
        return pl.ds(pl.multiple_of(start + n * TILES[p], 128), TILES[p])

    def tables_out(p, step, slot):
        return send(meta.at[p, spot(p, 0, step)], notes.at[p, slot], sm.at[p, step], rm.at[p, slot], peer(p, 0, step))

    def tokens_out(p, step, slot):
        return send(
            tok.at[:, columns_of(p)], gathered[p].at[slot], s1.at[p, step], r1.at[p, slot], peer(p, 0, step)
        )

    def picked_out(p, step, h, slot):
        return send(
            cut[p].at[spot(p, 1, step), h], relay[p].at[slot, h], s2.at[p, step, h], r2.at[p, slot, h], peer(p, 1, step)
        )

    def block_source(p, step):
        return cut[p] if step == 0 else relay[p]

    def block_out(p, step, h, way, slot):
        origin = spot(p, 1, step)
        return send(
            block_source(p, step).at[origin, h, spot(p, 2, way)], held[p].at[h, slot, origin],
            s3.at[p, step, h, way], r3.at[p, origin, h, slot], peer(p, 2, way, h),
        )

    def block_kept(p, step):
        origin = spot(p, 1, step)
        return pltpu.make_async_copy(
            block_source(p, step).at[origin, 0, mine(p, 2)], held[p].at[0, mine(p, 2), origin], keep.at[p, step]
        )

    def result_out(p, step, h, way, slot):
        owner = spot(p, 1, step)
        return send(
            held[p].at[h, spot(p, 2, way), owner], landed[p].at[owner, h, slot],
            t3.at[p, step, h, way], u3.at[p, owner, h, slot], peer(p, 2, way, h),
        )

    def result_kept(p, step):
        owner = spot(p, 1, step)
        return pltpu.make_async_copy(
            held[p].at[0, mine(p, 2), owner], landed[p].at[owner, 0, mine(p, 2)], keep_t.at[p, step]
        )

    def result_on(p, step, h, slot):
        return send(
            landed[p].at[spot(p, 1, step), h], home[p].at[slot, h], t2.at[p, step, h], u2.at[p, slot, h], peer(p, 1, step)
        )

    def fetched(p, step, h):
        origin = spot(p, 1, step)
        source = home[p] if step else landed[p]
        return pltpu.make_async_copy(source.at[origin, h], cut[p].at[origin, h], fetch.at[p, step, h])

    def sum_out(p, step, slot, n):
        columns = pl.ds(n * TILES[p], TILES[p])
        return send(
            gathered[p].at[spot(p, 0, step), :, columns], others[p].at[slot, :, columns],
            t1.at[p, step, n], u1.at[p, slot, n], peer(p, 0, step),
        )

    def ways(h):
        return RING + (0,) * h

    def forward(p, step, h):
        for way in ways(h):
            block_out(p, step, h, way, mine(p, 2)).start()
        if h == 0:
            block_kept(p, step).start()

    with jax.named_scope("send_tokens"):
        for step in RING:
            for p in range(3):
                tables_out(p, step, mine(p, 0)).start()
                tokens_out(p, step, mine(p, 0)).start()
        for p in range(3):
            gathered[p][mine(p, 0)] = tok[:, STARTS[p]:STARTS[p] + WIDTHS[p]]
            notes[p, mine(p, 0)] = meta[p, mine(p, 0)]

    def tabulate(p):
        for step in RING:
            tables_out(p, step, spot(p, 0, step)).wait_recv()
            tokens_out(p, step, spot(p, 0, step)).wait_recv()
        largest = jnp.maximum(jnp.maximum(notes[p, 0], notes[p, 1]), jnp.maximum(notes[p, 2], notes[p, 3]))
        total = notes[p, 0] + notes[p, 1] + notes[p, 2] + notes[p, 3]
        table = jnp.where(lax.broadcasted_iota(jnp.int32, (8, LANES), 0) < SIDE, largest, total)
        mixed[p] = table
        turned = table.T
        place = lax.broadcasted_iota(jnp.int32, (HALF // SIDE, SIDE * 128), 1).astype(F32)
        for h in range(CORES):
            for there in range(SIDE):
                column = turned[h * 160:(h + 1) * 160, there:there + 1]
                first = (2 * p + h) * 512
                full[there * 160:(there + 1) * 160, first:first + 512] = (column == place).astype(BF16)

    def pick(p, h):
        first = (2 * p + h) * 512

        @pl.loop(0, WIDTHS[p] // TILES[p])
        def _(n):
            rows = gathered[p][:, :, tile(p, n)].reshape(SIDE * 128, TILES[p])
            found = jnp.dot(full[:, first:first + 512], rows, preferred_element_type=F32)
            for b in range(SIDE * SIDE):
                block = found[b * BLOCK:(b + 1) * BLOCK].astype(BF16)
                cut[p][b // SIDE, h, b % SIDE, :, tile(p, n)] = block

    with jax.named_scope("pick_rows"):
        for p in range(3):
            tabulate(p)
            pick(p, 0)
            for step in RING:
                picked_out(p, step, 0, mine(p, 1)).start()
            forward(p, 0, 0)
        for p in range(3):
            pick(p, 1)

    with jax.named_scope("relay_rows"):
        for at, step in enumerate((3, 1, 2)):
            for p in range(3):
                picked_out(p, step, 0, spot(p, 1, step)).wait_recv()
                forward(p, step, 0)
                picked_out(p, RING[at], 1, mine(p, 1)).start()
        for p in range(3):
            forward(p, 0, 1)

    def relay_rows(step):
        for p in range(3):
            picked_out(p, step, 1, spot(p, 1, step)).wait_recv()
            forward(p, step, 1)

    def relay_results(step, h):
        for p in range(3):
            landing(p, step, h)
            result_on(p, step, h, mine(p, 1)).start()

    def arrive(h):
        for p in range(3):
            for step in range(SIDE):
                for way in ways(h):
                    block_out(p, step, h, way, spot(p, 2, way)).wait_recv()
                if h == 0:
                    block_kept(p, step).wait()

    def line_up(h):
        for p in range(3):
            @pl.loop(0, WIDTHS[p] // TILES[p])
            def _(n):
                rows = held[p][h, :, :, :, tile(p, n)].astype(F32).reshape(HALF, TILES[p]).astype(BF16)
                if p != 1:
                    rows = jnp.dot(turns[p // 2], rows, preferred_element_type=F32).astype(BF16)
                full[:, tile(p, n, STARTS[p])] = rows

    def hide(between):
        for n in range(4):
            columns = slice(n * 256, (n + 1) * 256)
            gate = jnp.dot(full[...], gate_w[:, columns], preferred_element_type=F32)
            lin = jnp.dot(full[...], up_w[:, columns], preferred_element_type=F32)
            hid[:, columns] = (gate * (1.0 / (1.0 + jnp.exp(-gate))) * lin).astype(BF16)
            if n:
                between(n)

    def answer(h, p):
        rows = hid if p == 1 else hid_t
        if p != 1:
            @pl.loop(0, 4)
            def _(n):
                columns = pl.ds(pl.multiple_of(n * 256, 128), 256)
                hid_t[:, columns] = jnp.dot(turns[1 - p // 2], hid[:, columns], preferred_element_type=F32).astype(BF16)

        @pl.loop(0, WIDTHS[p] // TILES[p])
        def _(n):
            result = jnp.dot(rows[...], down_w[:, tile(p, n, STARTS[p])], preferred_element_type=F32)
            for b in range(SIDE * SIDE):
                block = result[b * BLOCK:(b + 1) * BLOCK].astype(BF16)
                held[p][h, b // SIDE, b % SIDE, :, tile(p, n)] = block

        for step in RING + (0,):
            for way in ways(h):
                result_out(p, step, h, way, mine(p, 2)).start()
            if h == 0:
                result_kept(p, step).start()

    def landing(p, step, h):
        for way in ways(h):
            result_out(p, step, h, way, spot(p, 2, way)).wait_recv()
        if h == 0:
            result_kept(p, step).wait()

    with jax.named_scope("arrive_own"):
        arrive(0)
    with jax.named_scope("line_up"):
        loads[0].wait()
        line_up(0)
    with jax.named_scope("hidden"):
        loads[1].wait()
        loads[2].wait()
        hide(lambda n: relay_rows((3, 1, 2)[n - 1]))
    with jax.named_scope("answer"):
        loads[3].wait()
        for p in range(3):
            answer(0, p)
    with jax.named_scope("arrive_other"):
        arrive(1)
    with jax.named_scope("line_up"):
        line_up(1)
    with jax.named_scope("hidden"):
        hide(lambda n: relay_results(RING[n - 1], 0))
    with jax.named_scope("answer"):
        for p in range(3):
            answer(1, p)
    with jax.named_scope("wait_sent"):
        for p in range(3):
            for step in RING:
                tables_out(p, step, mine(p, 0)).wait_send()
                tokens_out(p, step, mine(p, 0)).wait_send()
                for h in range(CORES):
                    picked_out(p, step, h, mine(p, 1)).wait_send()
            for step in range(SIDE):
                for h in range(CORES):
                    for way in ways(h):
                        block_out(p, step, h, way, mine(p, 2)).wait_send()
    with jax.named_scope("fetch_own"):
        for p in range(3):
            landing(p, 0, 0)
            fetched(p, 0, 0).start()
        for step in (3, 1, 2):
            for p in range(3):
                result_on(p, step, 0, spot(p, 1, step)).wait_recv()
                fetched(p, step, 0).start()
    with jax.named_scope("relay_results_other"):
        for step in RING:
            relay_results(step, 1)
        for p in range(3):
            landing(p, 0, 1)
            fetched(p, 0, 1).start()

    def spread(p, there):
        at = p * SIDE + there
        ref, at = (full, at) if at < 9 else (hid, at - 9) if at < 11 else (hid_t, 0)
        return ref, slice(at * LANES, at * LANES + SLOTS)

    with jax.named_scope("spread_weights"):
        for p in range(3):
            token = lax.broadcasted_iota(jnp.int32, (SIDE * 128, SLOTS), 0).astype(F32)
            for there in range(SIDE):
                index = mixed[p, there:there + 1, :SLOTS]
                weight = mixed[p, SIDE + there:SIDE + there + 1, :SLOTS]
                ref, columns = spread(p, there)
                ref[:SIDE * 128, columns] = jnp.where(token == index, weight, 0.0).astype(BF16)
    with jax.named_scope("weighted_sum"):
        for step in (3, 1, 2):
            for p in range(3):
                result_on(p, step, 1, spot(p, 1, step)).wait_recv()
                fetched(p, step, 1).start()
        for n in range(max(w // t for w, t in zip(WIDTHS, TILES))):
            for p in range(3):
                if n >= WIDTHS[p] // TILES[p]:
                    continue
                if n == 0:
                    for step in range(SIDE):
                        for h in range(CORES):
                            fetched(p, step, h).wait()
                columns = slice(n * TILES[p], (n + 1) * TILES[p])
                total = jnp.zeros((SIDE * 128, TILES[p]), F32)
                for there in range(SIDE):
                    rows = cut[p][there, :, :, :, columns].astype(F32).reshape(SLOTS, TILES[p]).astype(BF16)
                    ref, of_slots = spread(p, there)
                    total = total + jnp.dot(ref[:SIDE * 128, of_slots], rows, preferred_element_type=F32)
                for k in range(SIDE):
                    gathered[p][k, :, columns] = total[k * 128:(k + 1) * 128].astype(BF16)
                for step in RING:
                    sum_out(p, step, mine(p, 0), n).start()
    with jax.named_scope("last_sum"):
        for n in range(max(w // t for w, t in zip(WIDTHS, TILES))):
            for p in range(3):
                if n >= WIDTHS[p] // TILES[p]:
                    continue
                columns = slice(n * TILES[p], (n + 1) * TILES[p])
                total = gathered[p][mine(p, 0), :, columns].astype(F32)
                for step in RING:
                    sum_out(p, step, spot(p, 0, step), n).wait_recv()
                    total = total + others[p][spot(p, 0, step), :, columns].astype(F32)
                out[:, STARTS[p] + n * TILES[p]:STARTS[p] + (n + 1) * TILES[p]] = total.astype(BF16)
    for p in range(3):
        for step in RING:
            for n in range(WIDTHS[p] // TILES[p]):
                sum_out(p, step, mine(p, 0), n).wait_send()
            for h in range(CORES):
                result_on(p, step, h, mine(p, 1)).wait_send()
        for step in range(SIDE):
            for h in range(CORES):
                for way in ways(h):
                    result_out(p, step, h, way, mine(p, 2)).wait_send()


ANY = pl.BlockSpec(memory_space=pl.ANY)
VMEM = pl.BlockSpec(memory_space=pltpu.VMEM)
DMA = pltpu.SemaphoreType.DMA


def blocks(leading):
    return [jax.ShapeDtypeStruct(leading + (w,), BF16) for w in WIDTHS]


def scratch(leading):
    return [pltpu.VMEM(leading + (w,), BF16) for w in WIDTHS]


def turn_matrices():
    row = jnp.arange(HALF, dtype=jnp.int32)
    k, i, j, s = row // 160, row // 40 % 4, row // 10 % 4, row % 10
    there = (i * 160 + j * 40 + k * 10 + s)[:, None] == row[None, :]
    return jnp.stack([there, there.T]).astype(BF16)


def tables(expert_ids, gate_weights):
    rows = expert_ids.shape[0]
    experts = SIDE ** 3 * CORES
    hit = expert_ids[:, :, None] == jnp.arange(experts, dtype=jnp.int32)[None, None, :]
    named = jnp.any(hit, axis=1)
    weight = jnp.sum(jnp.where(hit, gate_weights[:, :, None], 0.0), axis=1)
    below = (jnp.arange(rows)[:, None] > jnp.arange(rows)[None, :]).astype(BF16)
    place = jnp.dot(below, named.astype(BF16), preferred_element_type=F32).astype(jnp.int32)
    place = jnp.where(named, place, -1)
    pick = place.T[:, None, :] == jnp.arange(CAP, dtype=jnp.int32)[None, :, None]
    token = jnp.max(jnp.where(pick, jnp.arange(rows, dtype=jnp.int32).astype(F32)[None, None, :], -1.0), axis=2)
    amount = jnp.sum(jnp.where(pick, weight.T[:, None, :], 0.0), axis=2)
    shape = (SIDE, SIDE, SIDE, CORES, CAP)
    token, amount = token.reshape(shape), amount.reshape(shape)
    pos, core = whereabouts()
    token = jnp.where(core == 0, token, token[:, :, :, ::-1])
    amount = jnp.where(core == 0, amount, amount[:, :, :, ::-1])
    made = []
    for a1, a2, a3 in ORDERS:
        mine = (jnp.arange(SIDE) == pos[a1])[None, None, None, None, :, None]
        order = (a1, a2, 3, a3, 4)
        index = token.transpose(order)[:, :, :, :, None, :]
        index = jnp.where(mine & (index >= 0), index + (128 * pos[a1]).astype(F32), -1.0)
        value = jnp.where(mine, amount.transpose(order)[:, :, :, :, None, :], 0.0)
        index = jnp.pad(index.reshape(SIDE, SIDE, SLOTS), ((0, 0), (0, 0), (0, LANES - SLOTS)), constant_values=-1.0)
        value = jnp.pad(value.reshape(SIDE, SIDE, SLOTS), ((0, 0), (0, 0), (0, LANES - SLOTS)))
        made.append(jnp.concatenate([index, value], axis=1))
    return jnp.stack(made)


def body(tokens, expert_ids, gate_weights, w_gate, w_up, w_down):
    meta = tables(expert_ids, gate_weights)
    split = (SIDE, CORES, SIDE, BLOCK)
    out, *_ = pl.pallas_call(
        layer_kernel,
        out_shape=[jax.ShapeDtypeStruct(tokens.shape, BF16)] + blocks(split) * 3,
        in_specs=[VMEM, VMEM] + [ANY] * 4,
        out_specs=[VMEM] + [ANY] * 9,
        scratch_shapes=scratch((SIDE, 128)) + scratch(split) + scratch((CORES, SIDE, SIDE, BLOCK)) + scratch((SIDE, 128)) + [
            pltpu.VMEM(w_gate.shape[1:], BF16), pltpu.VMEM(w_up.shape[1:], BF16), pltpu.VMEM(w_down.shape[1:], BF16),
            pltpu.VMEM((2, HALF, HALF), BF16),
            pltpu.VMEM((HALF, tokens.shape[1]), BF16),
            pltpu.VMEM((HALF, w_gate.shape[2]), BF16),
            pltpu.VMEM((HALF, w_gate.shape[2]), BF16),
            pltpu.VMEM((3, SIDE, 8, LANES), F32),
            pltpu.VMEM((3, 8, LANES), F32),
        ] + [
            DMA((4,)), DMA((3, SIDE)), DMA((3, SIDE)), DMA((3, SIDE)), DMA((3, SIDE)),
            DMA((3, SIDE, CORES)), DMA((3, SIDE, CORES)), DMA((3, SIDE, CORES, SIDE)), DMA((3, SIDE, CORES, SIDE)),
            DMA((3, SIDE)), DMA((3, SIDE, CORES, SIDE)), DMA((3, SIDE, CORES, SIDE)), DMA((3, SIDE)),
            DMA((3, SIDE, CORES)), DMA((3, SIDE, CORES)), DMA((3, SIDE, CORES)), DMA((3, SIDE, 5)), DMA((3, SIDE, 5)),
        ],
        compiler_params=pltpu.CompilerParams(
            collective_id=0, has_side_effects=True, vmem_limit_bytes=62 * 2 ** 20
        ),
        name="layer",
    )(tokens, meta, w_gate[0], w_up[0], w_down[0], turn_matrices())
    return out


def solution(mesh):
    spec = P(("group", "local"), None)
    wide = P(("group", "local"), None, None)
    return jax.shard_map(
        body, mesh=mesh, in_specs=(spec, spec, spec, wide, wide, wide), out_specs=spec, check_vma=False
    )
```

```python
import jax
import jax.numpy as jnp
import numpy as np
from jax import lax
from jax.experimental import pallas as pl
from jax.experimental.pallas import tpu as pltpu
from jax.sharding import PartitionSpec as P

CAP = 10
SIDE = 4
CORES = 2
BLOCK = SIDE * CAP
SLOTS = SIDE * CORES * BLOCK
HALF = SIDE * SIDE * BLOCK
ORDERS = ((0, 1, 2), (1, 2, 0), (2, 0, 1))
WIDTHS = (1152, 1280, 1152)
STARTS = (0, 1152, 2432)
TILES = (384, 256, 384)
RING = (1, 3, 2)
PIECES = (((0, 384), (384, 768)), ((0, 512), (512, 768)), ((0, 384), (384, 768)))
BF16 = jnp.bfloat16
F32 = jnp.float32


def whereabouts():
    group, local = lax.axis_index("group"), lax.axis_index("local")
    return (group // SIDE, group % SIDE, local // CORES), local % CORES


def device_at(pos, core):
    return (pos[0] * SIDE + pos[1], pos[2] * CORES + core)


def along(pos, axis, value):
    return tuple(value if a == axis else pos[a] for a in range(3))


def greet(pos, core):
    barrier = pltpu.get_barrier_semaphore()
    peers = [device_at(pos, 1 - core)]
    for axis in range(3):
        for step in RING:
            for other in range(CORES):
                there = along(pos, axis, (pos[axis] + step) % SIDE)
                peers.append(device_at(there, (core + other) % CORES))
    for peer in peers:
        pl.semaphore_signal(barrier, inc=1, device_id=peer, device_id_type=pl.DeviceIdType.MESH)
    pl.semaphore_wait(barrier, len(peers))


def send(src, dst, send_sem, recv_sem, device):
    return pltpu.make_async_remote_copy(
        src_ref=src, dst_ref=dst, send_sem=send_sem, recv_sem=recv_sem,
        device_id=device, device_id_type=pl.DeviceIdType.MESH,
    )


def layer_kernel(tok, ids, amounts, sort, expand, lanes, wg, wu, wd, turn, out, ra, rb, rc, la, lb, lc, ha, hb, hc,
                 ga, gb, gc, sa, sb, sc, xa, xb, xc, qa, qb, qc, gate_w, up_w, down_w, turns, full, hid, hid_t, raw, tables, notes, mixed,
                 wsem, s1, r1, sm, rm, s2, r2, s3, r3, keep, t3, u3, keep_t, t2, u2, fetch, t1, u1):
    pos, core = whereabouts()
    gathered, cut, relay, held = (ga, gb, gc), (sa, sb, sc), (ra, rb, rc), (xa, xb, xc)
    landed, home, others = (la, lb, lc), (ha, hb, hc), (qa, qb, qc)
    loads = [
        pltpu.make_async_copy(a, b, wsem.at[i])
        for i, (a, b) in enumerate(((turn, turns), (wg, gate_w), (wu, up_w), (wd, down_w)))
    ]
    for copy in loads:
        copy.start()
    greet(pos, core)

    def spot(p, stage, step):
        return (pos[ORDERS[p][stage]] + step) % SIDE

    def mine(p, stage):
        return pos[ORDERS[p][stage]]

    def peer(p, stage, step, other=0):
        return device_at(along(pos, ORDERS[p][stage], spot(p, stage, step)), (core + other) % CORES)

    def tile(p, n, start=0):
        return pl.ds(pl.multiple_of(start + n * TILES[p], 128), TILES[p])

    def tables_out(p, step, slot):
        return send(tables.at[p, spot(p, 0, step)], notes.at[p, slot], sm.at[p, step], rm.at[p, slot], peer(p, 0, step))

    def tokens_out(p, step, slot, piece):
        first, width = PIECES[p][piece]
        return send(
            tok.at[:, pl.ds(STARTS[p] + first, width)], gathered[p].at[slot, :, pl.ds(first, width)],
            s1.at[p, step, piece], r1.at[p, slot, piece], peer(p, 0, step),
        )

    def picked_out(p, step, h, slot, piece):
        columns = pl.ds(*PIECES[p][piece])
        return send(
            cut[p].at[spot(p, 1, step), h, :, :, columns], relay[p].at[slot, h, :, :, columns],
            s2.at[p, step, h, piece], r2.at[p, slot, h, piece], peer(p, 1, step),
        )

    def block_source(p, step):
        return cut[p] if step == 0 else relay[p]

    def block_out(p, step, h, way, slot):
        origin = spot(p, 1, step)
        return send(
            block_source(p, step).at[origin, h, spot(p, 2, way)], held[p].at[h, slot, origin],
            s3.at[p, step, h, way], r3.at[p, origin, h, slot], peer(p, 2, way, h),
        )

    def block_kept(p, step):
        origin = spot(p, 1, step)
        return pltpu.make_async_copy(
            block_source(p, step).at[origin, 0, mine(p, 2)], held[p].at[0, mine(p, 2), origin], keep.at[p, step]
        )

    def result_out(p, step, h, way, slot):
        owner = spot(p, 1, step)
        return send(
            held[p].at[h, spot(p, 2, way), owner], landed[p].at[owner, h, slot],
            t3.at[p, step, h, way], u3.at[p, owner, h, slot], peer(p, 2, way, h),
        )

    def result_kept(p, step):
        owner = spot(p, 1, step)
        return pltpu.make_async_copy(
            held[p].at[0, mine(p, 2), owner], landed[p].at[owner, 0, mine(p, 2)], keep_t.at[p, step]
        )

    def result_on(p, step, h, slot):
        return send(
            landed[p].at[spot(p, 1, step), h], home[p].at[slot, h], t2.at[p, step, h], u2.at[p, slot, h], peer(p, 1, step)
        )

    def fetched(p, step, h):
        origin = spot(p, 1, step)
        source = home[p] if step else landed[p]
        return pltpu.make_async_copy(source.at[origin, h], cut[p].at[origin, h], fetch.at[p, step, h])

    def sum_out(p, step, slot, n):
        columns = pl.ds(n * TILES[p], TILES[p])
        return send(
            gathered[p].at[spot(p, 0, step), :, columns], others[p].at[slot, :, columns],
            t1.at[p, step, n], u1.at[p, slot, n], peer(p, 0, step),
        )

    def ways(h):
        return RING + (0,) * h

    def forward(p, step, h):
        for way in ways(h):
            block_out(p, step, h, way, mine(p, 2)).start()
        if h == 0:
            block_kept(p, step).start()

    def tokens_go(piece):
        for step in RING:
            for p in range(3):
                tokens_out(p, step, mine(p, 0), piece).start()

    def tokens_come(p, piece):
        for step in RING:
            tokens_out(p, step, spot(p, 0, step), piece).wait_recv()

    def make_tables():
        rows = tok.shape[0]
        lane = lax.broadcasted_iota(jnp.int32, (rows, 128), 1)
        token = lax.broadcasted_iota(jnp.int32, (rows, 128), 0)
        named, weight = jnp.zeros((rows, 128), F32), jnp.zeros((rows, 128), F32)
        for k in range(ids.shape[1]):
            hit = ids[:, k:k + 1] == lane
            named = jnp.where(hit, 1.0, named)
            weight = jnp.where(hit, amounts[:, k:k + 1], weight)
        before = jnp.dot((token > lane).astype(BF16), named.astype(BF16), preferred_element_type=F32)
        place = jnp.where(named > 0.0, before, -1.0)
        number = token.astype(F32) + 1.0
        slot = lax.broadcasted_iota(jnp.int32, (16, 128), 0)
        held_by, worth = jnp.zeros((16, 128), F32), jnp.zeros((16, 128), F32)
        for s in range(CAP):
            here = place == float(s)
            held_by = jnp.where(slot == s, jnp.max(jnp.where(here, number, 0.0), axis=0, keepdims=True), held_by)
            worth = jnp.where(slot == s, jnp.sum(jnp.where(here, weight, 0.0), axis=0, keepdims=True), worth)
        for p in range(3):
            raw[...] = jnp.zeros_like(raw)
            raw[pl.ds(pl.multiple_of(16 * mine(p, 0), 16), 16), :] = held_by
            raw[pl.ds(pl.multiple_of(64 + 16 * mine(p, 0), 16), 16), :] = worth
            sorted_rows = lax.dot_general(
                sort[p], raw[...].astype(BF16), (((1,), (1,)), ((), ())), preferred_element_type=F32
            )
            tables[p] = sorted_rows.astype(BF16).reshape(SIDE, 32, 128)

    def slot_columns(p, h):
        merged = notes[p, 0].astype(F32)
        for k in range(1, SIDE):
            merged = merged + notes[p, k].astype(F32)
        wide = jnp.dot(expand[(core + h) % CORES], merged.astype(BF16), preferred_element_type=F32)
        group = lax.broadcasted_iota(jnp.int32, (1, 128), 1) // 16 * 128
        own = wide * lanes[0].astype(F32)
        index = jnp.sum(own + jnp.where(own > 0.0, group.astype(F32), 0.0), axis=1, keepdims=True) - 1.0
        return index, jnp.sum(wide * lanes[1].astype(F32), axis=1, keepdims=True)

    def find(p, h):
        first = (2 * p + h) * 512
        place = lax.broadcasted_iota(jnp.int32, (HALF, SIDE * 128), 1).astype(F32)
        full[:, first:first + 512] = (slot_columns(p, h)[0] == place).astype(BF16)

    def turn_columns(p, h):
        index, weight = slot_columns(p, h)
        lane = lax.broadcasted_iota(jnp.int32, (HALF, 128), 1)
        mixed[p, h] = jnp.where(lane == 0, index, jnp.where(lane == 1, weight, 0.0)).T[:8]

    def pick(p, h, piece):
        first = (2 * p + h) * 512
        start, width = PIECES[p][piece]

        @pl.loop(0, width // TILES[p])
        def _(n):
            columns = tile(p, n, start)
            rows = gathered[p][:, :, columns].reshape(SIDE * 128, TILES[p])
            found = jnp.dot(full[:, first:first + 512], rows, preferred_element_type=F32)
            for b in range(SIDE * SIDE):
                block = found[b * BLOCK:(b + 1) * BLOCK].astype(BF16)
                cut[p][b // SIDE, h, b % SIDE, :, columns] = block

    with jax.named_scope("send_tokens"):
        tokens_go(0)
        make_tables()
        for step in RING:
            for p in range(3):
                tables_out(p, step, mine(p, 0)).start()
        tokens_go(1)
        for p in range(3):
            gathered[p][mine(p, 0)] = tok[:, STARTS[p]:STARTS[p] + WIDTHS[p]]
            notes[p, mine(p, 0)] = tables[p, mine(p, 0)]

    with jax.named_scope("pick_rows"):
        for p in range(3):
            for step in RING:
                tables_out(p, step, spot(p, 0, step)).wait_recv()
            find(p, 0)
        for piece in range(2):
            for p in range(3):
                tokens_come(p, piece)
                pick(p, 0, piece)
                for step in RING:
                    picked_out(p, step, 0, mine(p, 1), piece).start()
                if piece == 1:
                    forward(p, 0, 0)
        for p in range(3):
            find(p, 1)
            for piece in range(2):
                pick(p, 1, piece)

    with jax.named_scope("relay_rows"):
        for at, step in enumerate((3, 1, 2)):
            for p in range(3):
                for piece in range(2):
                    picked_out(p, step, 0, spot(p, 1, step), piece).wait_recv()
                forward(p, step, 0)
                for piece in range(2):
                    picked_out(p, RING[at], 1, mine(p, 1), piece).start()
        for p in range(3):
            forward(p, 0, 1)
        for p in range(3):
            for h in range(CORES):
                turn_columns(p, h)

    def relay_rows(step):
        for p in range(3):
            for piece in range(2):
                picked_out(p, step, 1, spot(p, 1, step), piece).wait_recv()
            forward(p, step, 1)

    def relay_results(step, h):
        for p in range(3):
            landing(p, step, h)
            result_on(p, step, h, mine(p, 1)).start()

    def arrive(h):
        for p in range(3):
            for step in range(SIDE):
                for way in ways(h):
                    block_out(p, step, h, way, spot(p, 2, way)).wait_recv()
                if h == 0:
                    block_kept(p, step).wait()

    def line_up(h):
        for p in range(3):
            @pl.loop(0, WIDTHS[p] // TILES[p])
            def _(n):
                rows = held[p][h, :, :, :, tile(p, n)].astype(F32).reshape(HALF, TILES[p]).astype(BF16)
                if p != 1:
                    rows = jnp.dot(turns[p // 2], rows, preferred_element_type=F32).astype(BF16)
                full[:, tile(p, n, STARTS[p])] = rows

    def hide(between):
        for n in range(4):
            columns = slice(n * 256, (n + 1) * 256)
            gate = jnp.dot(full[...], gate_w[:, columns], preferred_element_type=F32)
            lin = jnp.dot(full[...], up_w[:, columns], preferred_element_type=F32)
            hid[:, columns] = (gate * (1.0 / (1.0 + jnp.exp(-gate))) * lin).astype(BF16)
            if n:
                between(n)

    def answer(h, p):
        rows = hid if p == 1 else hid_t
        if p != 1:
            @pl.loop(0, 4)
            def _(n):
                columns = pl.ds(pl.multiple_of(n * 256, 128), 256)
                hid_t[:, columns] = jnp.dot(turns[1 - p // 2], hid[:, columns], preferred_element_type=F32).astype(BF16)

        @pl.loop(0, WIDTHS[p] // TILES[p])
        def _(n):
            result = jnp.dot(rows[...], down_w[:, tile(p, n, STARTS[p])], preferred_element_type=F32)
            for b in range(SIDE * SIDE):
                block = result[b * BLOCK:(b + 1) * BLOCK].astype(BF16)
                held[p][h, b // SIDE, b % SIDE, :, tile(p, n)] = block

        for step in RING + (0,):
            for way in ways(h):
                result_out(p, step, h, way, mine(p, 2)).start()
            if h == 0:
                result_kept(p, step).start()

    def landing(p, step, h):
        for way in ways(h):
            result_out(p, step, h, way, spot(p, 2, way)).wait_recv()
        if h == 0:
            result_kept(p, step).wait()

    with jax.named_scope("arrive_own"):
        arrive(0)
    with jax.named_scope("line_up"):
        loads[0].wait()
        line_up(0)
    with jax.named_scope("hidden"):
        loads[1].wait()
        loads[2].wait()
        hide(lambda n: relay_rows((3, 1, 2)[n - 1]))
    with jax.named_scope("answer"):
        loads[3].wait()
        for p in range(3):
            answer(0, p)
    with jax.named_scope("arrive_other"):
        arrive(1)
    with jax.named_scope("line_up"):
        line_up(1)
    with jax.named_scope("hidden"):
        hide(lambda n: relay_results(RING[n - 1], 0))
    with jax.named_scope("answer"):
        for p in range(3):
            answer(1, p)
    with jax.named_scope("wait_sent"):
        for p in range(3):
            for step in RING:
                tables_out(p, step, mine(p, 0)).wait_send()
                for piece in range(2):
                    tokens_out(p, step, mine(p, 0), piece).wait_send()
                    for h in range(CORES):
                        picked_out(p, step, h, mine(p, 1), piece).wait_send()
            for step in range(SIDE):
                for h in range(CORES):
                    for way in ways(h):
                        block_out(p, step, h, way, mine(p, 2)).wait_send()
    with jax.named_scope("fetch_own"):
        for p in range(3):
            landing(p, 0, 0)
            fetched(p, 0, 0).start()
        for step in (3, 1, 2):
            for p in range(3):
                result_on(p, step, 0, spot(p, 1, step)).wait_recv()
                fetched(p, step, 0).start()
    with jax.named_scope("relay_results_other"):
        for step in RING:
            relay_results(step, 1)
        for p in range(3):
            landing(p, 0, 1)
            fetched(p, 0, 1).start()

    def spread(p, h):
        if p < 2:
            return full, slice((2 * p + h) * HALF, (2 * p + h + 1) * HALF)
        return (hid, hid_t)[h], slice(0, HALF)

    with jax.named_scope("spread_weights"):
        token = lax.broadcasted_iota(jnp.int32, (SIDE * 128, HALF), 0).astype(F32)
        for p in range(3):
            for h in range(CORES):
                ref, columns = spread(p, h)
                ref[:SIDE * 128, columns] = jnp.where(token == mixed[p, h, 0:1], mixed[p, h, 1:2], 0.0).astype(BF16)
    with jax.named_scope("weighted_sum"):
        for step in (3, 1, 2):
            for p in range(3):
                result_on(p, step, 1, spot(p, 1, step)).wait_recv()
                fetched(p, step, 1).start()
        for n in range(max(w // t for w, t in zip(WIDTHS, TILES))):
            for p in range(3):
                if n >= WIDTHS[p] // TILES[p]:
                    continue
                if n == 0:
                    for step in range(SIDE):
                        for h in range(CORES):
                            fetched(p, step, h).wait()
                columns = slice(n * TILES[p], (n + 1) * TILES[p])
                total = jnp.zeros((SIDE * 128, TILES[p]), F32)
                for h in range(CORES):
                    rows = cut[p][:, h, :, :, columns].astype(F32).reshape(HALF, TILES[p]).astype(BF16)
                    ref, of_slots = spread(p, h)
                    total = total + jnp.dot(ref[:SIDE * 128, of_slots], rows, preferred_element_type=F32)
                for k in range(SIDE):
                    gathered[p][k, :, columns] = total[k * 128:(k + 1) * 128].astype(BF16)
                for step in RING:
                    sum_out(p, step, mine(p, 0), n).start()
    with jax.named_scope("last_sum"):
        for n in range(max(w // t for w, t in zip(WIDTHS, TILES))):
            for p in range(3):
                if n >= WIDTHS[p] // TILES[p]:
                    continue
                columns = slice(n * TILES[p], (n + 1) * TILES[p])
                total = gathered[p][mine(p, 0), :, columns].astype(F32)
                for step in RING:
                    sum_out(p, step, spot(p, 0, step), n).wait_recv()
                    total = total + others[p][spot(p, 0, step), :, columns].astype(F32)
                out[:, STARTS[p] + n * TILES[p]:STARTS[p] + (n + 1) * TILES[p]] = total.astype(BF16)
    for p in range(3):
        for step in RING:
            for n in range(WIDTHS[p] // TILES[p]):
                sum_out(p, step, mine(p, 0), n).wait_send()
            for h in range(CORES):
                result_on(p, step, h, mine(p, 1)).wait_send()
        for step in range(SIDE):
            for h in range(CORES):
                for way in ways(h):
                    result_out(p, step, h, way, mine(p, 2)).wait_send()


ANY = pl.BlockSpec(memory_space=pl.ANY)
VMEM = pl.BlockSpec(memory_space=pltpu.VMEM)
DMA = pltpu.SemaphoreType.DMA


def blocks(leading):
    return [jax.ShapeDtypeStruct(leading + (w,), BF16) for w in WIDTHS]


def scratch(leading):
    return [pltpu.VMEM(leading + (w,), BF16) for w in WIDTHS]


def constants():
    row = np.arange(HALF)
    k, i, j, s = row // 160, row // 40 % 4, row // 10 % 4, row % 10
    there = (i * 160 + j * 40 + k * 10 + s)[:, None] == row[None, :]
    turn = np.stack([there, there.T])
    expert = np.arange(SIDE ** 3 * CORES).reshape(SIDE, SIDE, SIDE, CORES)
    sort = np.stack([expert.transpose(*order, 3).reshape(-1)[:, None] == np.arange(expert.size) for order in ORDERS])
    expand = np.stack([((row // 40) * CORES + core)[:, None] == np.arange(32) for core in range(CORES)])
    lane = (j * 16 + s)[:, None]
    lanes = np.stack([lane == np.arange(128), lane + 64 == np.arange(128)])
    return tuple(jnp.asarray(a.astype(np.float32), dtype=BF16) for a in (sort, expand, lanes, turn))


def body(tokens, expert_ids, gate_weights, w_gate, w_up, w_down):
    sort, expand, lanes, turn = constants()
    split = (SIDE, CORES, SIDE, BLOCK)
    out, *_ = pl.pallas_call(
        layer_kernel,
        out_shape=[jax.ShapeDtypeStruct(tokens.shape, BF16)] + blocks(split) * 3,
        in_specs=[VMEM] * 6 + [ANY] * 4,
        out_specs=[VMEM] + [ANY] * 9,
        scratch_shapes=scratch((SIDE, 128)) + scratch(split) + scratch((CORES, SIDE, SIDE, BLOCK)) + scratch((SIDE, 128)) + [
            pltpu.VMEM(w_gate.shape[1:], BF16), pltpu.VMEM(w_up.shape[1:], BF16), pltpu.VMEM(w_down.shape[1:], BF16),
            pltpu.VMEM((2, HALF, HALF), BF16),
            pltpu.VMEM((HALF, tokens.shape[1]), BF16),
            pltpu.VMEM((HALF, w_gate.shape[2]), BF16),
            pltpu.VMEM((HALF, w_gate.shape[2]), BF16),
            pltpu.VMEM((128, 128), F32),
            pltpu.VMEM((3, SIDE, 32, 128), BF16),
            pltpu.VMEM((3, SIDE, 32, 128), BF16),
            pltpu.VMEM((3, CORES, 8, HALF), F32),
        ] + [
            DMA((4,)), DMA((3, SIDE, 2)), DMA((3, SIDE, 2)), DMA((3, SIDE)), DMA((3, SIDE)),
            DMA((3, SIDE, CORES, 2)), DMA((3, SIDE, CORES, 2)), DMA((3, SIDE, CORES, SIDE)), DMA((3, SIDE, CORES, SIDE)),
            DMA((3, SIDE)), DMA((3, SIDE, CORES, SIDE)), DMA((3, SIDE, CORES, SIDE)), DMA((3, SIDE)),
            DMA((3, SIDE, CORES)), DMA((3, SIDE, CORES)), DMA((3, SIDE, CORES)), DMA((3, SIDE, 5)), DMA((3, SIDE, 5)),
        ],
        compiler_params=pltpu.CompilerParams(
            collective_id=0, has_side_effects=True, vmem_limit_bytes=62 * 2 ** 20
        ),
        name="layer",
    )(tokens, expert_ids, gate_weights, sort, expand, lanes, w_gate[0], w_up[0], w_down[0], turn)
    return out


def solution(mesh):
    spec = P(("group", "local"), None)
    wide = P(("group", "local"), None, None)
    return jax.shard_map(
        body, mesh=mesh, in_specs=(spec, spec, spec, wide, wide, wide), out_specs=spec, check_vma=False
    )
```

```python
import jax
import jax.numpy as jnp
import numpy as np
from jax import lax
from jax.experimental import pallas as pl
from jax.experimental.pallas import tpu as pltpu
from jax.sharding import PartitionSpec as P

CAP = 10
SIDE = 4
CORES = 2
BLOCK = SIDE * CAP
SLOTS = SIDE * CORES * BLOCK
HALF = SIDE * SIDE * BLOCK
ORDERS = ((0, 1, 2), (1, 2, 0), (2, 0, 1))
WIDTHS = (1152, 1280, 1152)
STARTS = (0, 1152, 2432)
TILES = (384, 256, 384)
RING = (1, 3, 2)
PIECES = (((0, 384), (384, 768)), ((0, 512), (512, 768)), ((0, 384), (384, 768)))
BF16 = jnp.bfloat16
F32 = jnp.float32


def whereabouts():
    group, local = lax.axis_index("group"), lax.axis_index("local")
    return (group // SIDE, group % SIDE, local // CORES), local % CORES


def device_at(pos, core):
    return (pos[0] * SIDE + pos[1], pos[2] * CORES + core)


def along(pos, axis, value):
    return tuple(value if a == axis else pos[a] for a in range(3))


def greet(pos, core):
    barrier = pltpu.get_barrier_semaphore()
    peers = [device_at(pos, 1 - core)]
    for axis in range(3):
        for step in RING:
            for other in range(CORES):
                there = along(pos, axis, (pos[axis] + step) % SIDE)
                peers.append(device_at(there, (core + other) % CORES))
    for peer in peers:
        pl.semaphore_signal(barrier, inc=1, device_id=peer, device_id_type=pl.DeviceIdType.MESH)
    pl.semaphore_wait(barrier, len(peers))


def send(src, dst, send_sem, recv_sem, device):
    return pltpu.make_async_remote_copy(
        src_ref=src, dst_ref=dst, send_sem=send_sem, recv_sem=recv_sem,
        device_id=device, device_id_type=pl.DeviceIdType.MESH,
    )


def layer_kernel(tok, ids, amounts, sort, expand, lanes, wg, wu, wd, turn, out, ra, rb, rc, la, lb, lc, ha, hb, hc,
                 ga, gb, gc, sa, sb, sc, xa, xb, xc, qa, qb, qc, gate_w, up_w, down_w, turns, full, hid, hid_t, raw, tables, notes, mixed,
                 wsem, s1, r1, sm, rm, s2, r2, s3, r3, keep, t3, u3, keep_t, t2, u2, fetch, t1, u1):
    pos, core = whereabouts()
    gathered, cut, relay, held = (ga, gb, gc), (sa, sb, sc), (ra, rb, rc), (xa, xb, xc)
    landed, home, others = (la, lb, lc), (ha, hb, hc), (qa, qb, qc)
    loads = [
        pltpu.make_async_copy(a, b, wsem.at[i])
        for i, (a, b) in enumerate(((turn, turns), (wg, gate_w), (wu, up_w), (wd, down_w)))
    ]
    for copy in loads:
        copy.start()
    greet(pos, core)

    def spot(p, stage, step):
        return (pos[ORDERS[p][stage]] + step) % SIDE

    def mine(p, stage):
        return pos[ORDERS[p][stage]]

    def peer(p, stage, step, other=0):
        return device_at(along(pos, ORDERS[p][stage], spot(p, stage, step)), (core + other) % CORES)

    def tile(p, n, start=0):
        return pl.ds(pl.multiple_of(start + n * TILES[p], 128), TILES[p])

    def tables_out(p, step, slot):
        return send(tables.at[p, spot(p, 0, step)], notes.at[p, slot], sm.at[p], rm.at[p], peer(p, 0, step))

    def tokens_out(p, step, slot, piece):
        first, width = PIECES[p][piece]
        return send(
            tok.at[:, pl.ds(STARTS[p] + first, width)], gathered[p].at[slot, :, pl.ds(first, width)],
            s1.at[p], r1.at[p, slot, piece], peer(p, 0, step),
        )

    def picked_out(p, step, h, slot, piece):
        columns = pl.ds(*PIECES[p][piece])
        return send(
            cut[p].at[spot(p, 1, step), h, :, :, columns], relay[p].at[slot, h, :, :, columns],
            s2.at[p, h], r2.at[p, slot, h], peer(p, 1, step),
        )

    def block_source(p, step):
        return cut[p] if step == 0 else relay[p]

    def block_out(p, step, h, way, slot):
        origin = spot(p, 1, step)
        return send(
            block_source(p, step).at[origin, h, spot(p, 2, way)], held[p].at[h, slot, origin],
            s3.at[p, h], r3.at[p, h], peer(p, 2, way, h),
        )

    def block_kept(p, step):
        origin = spot(p, 1, step)
        return pltpu.make_async_copy(
            block_source(p, step).at[origin, 0, mine(p, 2)], held[p].at[0, mine(p, 2), origin], keep.at[p]
        )

    def result_out(p, step, h, way, slot):
        owner = spot(p, 1, step)
        return send(
            held[p].at[h, spot(p, 2, way), owner], landed[p].at[owner, h, slot],
            t3.at[p, h], u3.at[p, owner, h], peer(p, 2, way, h),
        )

    def result_kept(p, step):
        owner = spot(p, 1, step)
        return pltpu.make_async_copy(
            held[p].at[0, mine(p, 2), owner], landed[p].at[owner, 0, mine(p, 2)], keep_t.at[p, step]
        )

    def result_on(p, step, h, slot):
        return send(
            landed[p].at[spot(p, 1, step), h], home[p].at[slot, h], t2.at[p, h], u2.at[p, slot, h], peer(p, 1, step)
        )

    def fetched(p, step, h):
        origin = spot(p, 1, step)
        source = home[p] if step else landed[p]
        return pltpu.make_async_copy(source.at[origin, h], cut[p].at[origin, h], fetch.at[p])

    def sum_out(p, step, slot, n):
        columns = pl.ds(n * TILES[p], TILES[p])
        return send(
            gathered[p].at[spot(p, 0, step), :, columns], others[p].at[slot, :, columns],
            t1.at[p], u1.at[p, n], peer(p, 0, step),
        )

    def await_bytes(ref, sem):
        pltpu.make_async_copy(ref, ref, sem).wait()

    def blocks_of(p, h):
        return held[p].at[h, pl.ds(0, SIDE - 1 + h)]

    def ways(h):
        return RING + (0,) * h

    def forward(p, step, h):
        for way in ways(h):
            block_out(p, step, h, way, mine(p, 2)).start()
        if h == 0:
            block_kept(p, step).start()

    def tokens_go(piece):
        for step in RING:
            for p in range(3):
                tokens_out(p, step, mine(p, 0), piece).start()

    def tokens_come(p, piece):
        for step in RING:
            tokens_out(p, step, spot(p, 0, step), piece).wait_recv()

    def make_tables():
        rows = tok.shape[0]
        lane = lax.broadcasted_iota(jnp.int32, (rows, 128), 1)
        token = lax.broadcasted_iota(jnp.int32, (rows, 128), 0)
        named, weight = jnp.zeros((rows, 128), F32), jnp.zeros((rows, 128), F32)
        experts, worths = ids[...].astype(F32).T, amounts[...].T
        for k in range(ids.shape[0]):
            hit = experts[:, k:k + 1] == lane.astype(F32)
            named = jnp.where(hit, 1.0, named)
            weight = jnp.where(hit, worths[:, k:k + 1], weight)
        before = jnp.dot((token > lane).astype(BF16), named.astype(BF16), preferred_element_type=F32)
        place = jnp.where(named > 0.0, before, -1.0)
        number = token.astype(F32) + 1.0
        slot = lax.broadcasted_iota(jnp.int32, (16, 128), 0)
        held_by, worth = jnp.zeros((16, 128), F32), jnp.zeros((16, 128), F32)
        for s in range(CAP):
            here = place == float(s)
            held_by = jnp.where(slot == s, jnp.max(jnp.where(here, number, 0.0), axis=0, keepdims=True), held_by)
            worth = jnp.where(slot == s, jnp.sum(jnp.where(here, weight, 0.0), axis=0, keepdims=True), worth)
        for p in range(3):
            raw[...] = jnp.zeros_like(raw)
            raw[pl.ds(pl.multiple_of(16 * mine(p, 0), 16), 16), :] = held_by
            raw[pl.ds(pl.multiple_of(64 + 16 * mine(p, 0), 16), 16), :] = worth
            sorted_rows = lax.dot_general(
                sort[p], raw[...].astype(BF16), (((1,), (1,)), ((), ())), preferred_element_type=F32
            )
            tables[p] = sorted_rows.astype(BF16).reshape(SIDE, 32, 128)

    def slot_columns(p, h):
        merged = notes[p, 0].astype(F32)
        for k in range(1, SIDE):
            merged = merged + notes[p, k].astype(F32)
        wide = jnp.dot(expand[(core + h) % CORES], merged.astype(BF16), preferred_element_type=F32)
        group = lax.broadcasted_iota(jnp.int32, (1, 128), 1) // 16 * 128
        own = wide * lanes[0].astype(F32)
        index = jnp.sum(own + jnp.where(own > 0.0, group.astype(F32), 0.0), axis=1, keepdims=True) - 1.0
        return index, jnp.sum(wide * lanes[1].astype(F32), axis=1, keepdims=True)

    def find(p, h):
        first = (2 * p + h) * 512
        place = lax.broadcasted_iota(jnp.int32, (HALF, SIDE * 128), 1).astype(F32)
        full[:, first:first + 512] = (slot_columns(p, h)[0] == place).astype(BF16)

    def turn_columns(p, h):
        index, weight = slot_columns(p, h)
        lane = lax.broadcasted_iota(jnp.int32, (HALF, 128), 1)
        mixed[p, h] = jnp.where(lane == 0, index, jnp.where(lane == 1, weight, 0.0)).T[:8]

    def pick(p, h, piece):
        first = (2 * p + h) * 512
        start, width = PIECES[p][piece]

        @pl.loop(0, width // TILES[p])
        def _(n):
            columns = tile(p, n, start)
            rows = gathered[p][:, :, columns].reshape(SIDE * 128, TILES[p])
            found = jnp.dot(full[:, first:first + 512], rows, preferred_element_type=F32)
            for b in range(SIDE * SIDE):
                block = found[b * BLOCK:(b + 1) * BLOCK].astype(BF16)
                cut[p][b // SIDE, h, b % SIDE, :, columns] = block

    with jax.named_scope("send_tokens"):
        tokens_go(0)
        make_tables()
        for step in RING:
            for p in range(3):
                tables_out(p, step, mine(p, 0)).start()
        tokens_go(1)
        for p in range(3):
            gathered[p][mine(p, 0)] = tok[:, STARTS[p]:STARTS[p] + WIDTHS[p]]
            notes[p, mine(p, 0)] = tables[p, mine(p, 0)]

    with jax.named_scope("pick_rows"):
        for p in range(3):
            await_bytes(notes.at[p, pl.ds(0, SIDE - 1)], rm.at[p])
            find(p, 0)
        for piece in range(2):
            for p in range(3):
                tokens_come(p, piece)
                pick(p, 0, piece)
                for step in RING:
                    picked_out(p, step, 0, mine(p, 1), piece).start()
                if piece == 1:
                    forward(p, 0, 0)
        for p in range(3):
            find(p, 1)
            for piece in range(2):
                pick(p, 1, piece)

    with jax.named_scope("relay_rows"):
        for at, step in enumerate((3, 1, 2)):
            for p in range(3):
                await_bytes(relay[p].at[spot(p, 1, step), 0], r2.at[p, spot(p, 1, step), 0])
                forward(p, step, 0)
                for piece in range(2):
                    picked_out(p, RING[at], 1, mine(p, 1), piece).start()
        for p in range(3):
            forward(p, 0, 1)
        for p in range(3):
            for h in range(CORES):
                turn_columns(p, h)

    def relay_rows(step):
        for p in range(3):
            await_bytes(relay[p].at[spot(p, 1, step), 1], r2.at[p, spot(p, 1, step), 1])
            forward(p, step, 1)

    def relay_results(step, h):
        for p in range(3):
            landing(p, step, h)
            result_on(p, step, h, mine(p, 1)).start()

    def arrive(h):
        for p in range(3):
            await_bytes(blocks_of(p, h), r3.at[p, h])
            if h == 0:
                await_bytes(held[p].at[0, 0], keep.at[p])

    def line_up(h):
        for p in range(3):
            @pl.loop(0, WIDTHS[p] // TILES[p])
            def _(n):
                rows = held[p][h, :, :, :, tile(p, n)].astype(F32).reshape(HALF, TILES[p]).astype(BF16)
                if p != 1:
                    rows = jnp.dot(turns[p // 2], rows, preferred_element_type=F32).astype(BF16)
                full[:, tile(p, n, STARTS[p])] = rows

    def hide(between):
        for n in range(4):
            columns = slice(n * 256, (n + 1) * 256)
            gate = jnp.dot(full[...], gate_w[:, columns], preferred_element_type=F32)
            lin = jnp.dot(full[...], up_w[:, columns], preferred_element_type=F32)
            hid[:, columns] = (gate * (1.0 / (1.0 + jnp.exp(-gate))) * lin).astype(BF16)
            if n:
                between(n)

    def answer(h, p):
        rows = hid if p == 1 else hid_t
        if p != 1:
            @pl.loop(0, 4)
            def _(n):
                columns = pl.ds(pl.multiple_of(n * 256, 128), 256)
                hid_t[:, columns] = jnp.dot(turns[1 - p // 2], hid[:, columns], preferred_element_type=F32).astype(BF16)

        @pl.loop(0, WIDTHS[p] // TILES[p])
        def _(n):
            result = jnp.dot(rows[...], down_w[:, tile(p, n, STARTS[p])], preferred_element_type=F32)
            for b in range(SIDE * SIDE):
                block = result[b * BLOCK:(b + 1) * BLOCK].astype(BF16)
                held[p][h, b // SIDE, b % SIDE, :, tile(p, n)] = block

        for step in RING + (0,):
            for way in ways(h):
                result_out(p, step, h, way, mine(p, 2)).start()
            if h == 0:
                result_kept(p, step).start()

    def landing(p, step, h):
        owner = spot(p, 1, step)
        await_bytes(landed[p].at[owner, h, pl.ds(0, SIDE - 1 + h)], u3.at[p, owner, h])
        if h == 0:
            result_kept(p, step).wait()

    with jax.named_scope("arrive_own"):
        arrive(0)
    with jax.named_scope("line_up"):
        loads[0].wait()
        line_up(0)
    with jax.named_scope("hidden"):
        loads[1].wait()
        loads[2].wait()
        hide(lambda n: relay_rows((3, 1, 2)[n - 1]))
    with jax.named_scope("answer"):
        loads[3].wait()
        for p in (1, 0, 2):
            answer(0, p)
    with jax.named_scope("arrive_other"):
        arrive(1)
    with jax.named_scope("line_up"):
        line_up(1)
    with jax.named_scope("hidden"):
        hide(lambda n: relay_results(RING[n - 1], 0))
    with jax.named_scope("answer"):
        for p in (1, 0, 2):
            answer(1, p)
    with jax.named_scope("wait_sent"):
        for p in range(3):
            await_bytes(notes.at[p, pl.ds(0, SIDE - 1)], sm.at[p])
            await_bytes(gathered[p].at[pl.ds(0, SIDE - 1)], s1.at[p])
            for h in range(CORES):
                await_bytes(blocks_of(p, 0), s2.at[p, h])
                await_bytes(blocks_of(p, h), s3.at[p, h])
    with jax.named_scope("fetch_own"):
        for p in range(3):
            landing(p, 0, 0)
            fetched(p, 0, 0).start()
        for step in (3, 1, 2):
            for p in range(3):
                result_on(p, step, 0, spot(p, 1, step)).wait_recv()
                fetched(p, step, 0).start()
    with jax.named_scope("relay_results_other"):
        for step in RING:
            relay_results(step, 1)
        for p in range(3):
            landing(p, 0, 1)
            fetched(p, 0, 1).start()

    def spread(p, h):
        if p < 2:
            return full, slice((2 * p + h) * HALF, (2 * p + h + 1) * HALF)
        return (hid, hid_t)[h], slice(0, HALF)

    with jax.named_scope("spread_weights"):
        token = lax.broadcasted_iota(jnp.int32, (SIDE * 128, HALF), 0).astype(F32)
        for p in range(3):
            for h in range(CORES):
                ref, columns = spread(p, h)
                ref[:SIDE * 128, columns] = jnp.where(token == mixed[p, h, 0:1], mixed[p, h, 1:2], 0.0).astype(BF16)
    with jax.named_scope("weighted_sum"):
        for step in (3, 1, 2):
            for p in range(3):
                result_on(p, step, 1, spot(p, 1, step)).wait_recv()
                fetched(p, step, 1).start()
        for n in range(max(w // t for w, t in zip(WIDTHS, TILES))):
            for p in range(3):
                if n >= WIDTHS[p] // TILES[p]:
                    continue
                if n == 0:
                    await_bytes(cut[p], fetch.at[p])
                columns = slice(n * TILES[p], (n + 1) * TILES[p])
                total = jnp.zeros((SIDE * 128, TILES[p]), F32)
                for h in range(CORES):
                    rows = cut[p][:, h, :, :, columns].astype(F32).reshape(HALF, TILES[p]).astype(BF16)
                    ref, of_slots = spread(p, h)
                    total = total + jnp.dot(ref[:SIDE * 128, of_slots], rows, preferred_element_type=F32)
                for k in range(SIDE):
                    gathered[p][k, :, columns] = total[k * 128:(k + 1) * 128].astype(BF16)
                for step in RING:
                    sum_out(p, step, mine(p, 0), n).start()
    with jax.named_scope("last_sum"):
        for n in range(max(w // t for w, t in zip(WIDTHS, TILES))):
            for p in range(3):
                if n >= WIDTHS[p] // TILES[p]:
                    continue
                columns = slice(n * TILES[p], (n + 1) * TILES[p])
                total = gathered[p][mine(p, 0), :, columns].astype(F32)
                await_bytes(others[p].at[pl.ds(0, SIDE - 1), :, columns], u1.at[p, n])
                for step in RING:
                    total = total + others[p][spot(p, 0, step), :, columns].astype(F32)
                out[:, STARTS[p] + n * TILES[p]:STARTS[p] + (n + 1) * TILES[p]] = total.astype(BF16)
    for p in range(3):
        await_bytes(gathered[p].at[pl.ds(0, SIDE - 1)], t1.at[p])
        for h in range(CORES):
            await_bytes(blocks_of(p, 0), t2.at[p, h])
            await_bytes(blocks_of(p, h), t3.at[p, h])


ANY = pl.BlockSpec(memory_space=pl.ANY)
VMEM = pl.BlockSpec(memory_space=pltpu.VMEM)
DMA = pltpu.SemaphoreType.DMA


def blocks(leading):
    return [jax.ShapeDtypeStruct(leading + (w,), BF16) for w in WIDTHS]


def scratch(leading):
    return [pltpu.VMEM(leading + (w,), BF16) for w in WIDTHS]


def constants():
    row = np.arange(HALF)
    k, i, j, s = row // 160, row // 40 % 4, row // 10 % 4, row % 10
    there = (i * 160 + j * 40 + k * 10 + s)[:, None] == row[None, :]
    turn = np.stack([there, there.T])
    expert = np.arange(SIDE ** 3 * CORES).reshape(SIDE, SIDE, SIDE, CORES)
    sort = np.stack([expert.transpose(*order, 3).reshape(-1)[:, None] == np.arange(expert.size) for order in ORDERS])
    expand = np.stack([((row // 40) * CORES + core)[:, None] == np.arange(32) for core in range(CORES)])
    lane = (j * 16 + s)[:, None]
    lanes = np.stack([lane == np.arange(128), lane + 64 == np.arange(128)])
    return tuple(jnp.asarray(a.astype(np.float32), dtype=BF16) for a in (sort, expand, lanes, turn))


def body(tokens, expert_ids, gate_weights, w_gate, w_up, w_down):
    sort, expand, lanes, turn = constants()
    split = (SIDE, CORES, SIDE, BLOCK)
    out, *_ = pl.pallas_call(
        layer_kernel,
        out_shape=[jax.ShapeDtypeStruct(tokens.shape, BF16)] + blocks(split) * 3,
        in_specs=[VMEM] * 6 + [ANY] * 4,
        out_specs=[VMEM] + [ANY] * 9,
        scratch_shapes=scratch((SIDE, 128)) + scratch(split) + scratch((CORES, SIDE, SIDE, BLOCK)) + scratch((SIDE, 128)) + [
            pltpu.VMEM(w_gate.shape[1:], BF16), pltpu.VMEM(w_up.shape[1:], BF16), pltpu.VMEM(w_down.shape[1:], BF16),
            pltpu.VMEM((2, HALF, HALF), BF16),
            pltpu.VMEM((HALF, tokens.shape[1]), BF16),
            pltpu.VMEM((HALF, w_gate.shape[2]), BF16),
            pltpu.VMEM((HALF, w_gate.shape[2]), BF16),
            pltpu.VMEM((128, 128), F32),
            pltpu.VMEM((3, SIDE, 32, 128), BF16),
            pltpu.VMEM((3, SIDE, 32, 128), BF16),
            pltpu.VMEM((3, CORES, 8, HALF), F32),
        ] + [
            DMA((4,)), DMA((3,)), DMA((3, SIDE, 2)), DMA((3,)), DMA((3,)),
            DMA((3, CORES)), DMA((3, SIDE, CORES)), DMA((3, CORES)), DMA((3, CORES)), DMA((3,)),
            DMA((3, CORES)), DMA((3, SIDE, CORES)), DMA((3, SIDE)), DMA((3, CORES)), DMA((3, SIDE, CORES)),
            DMA((3,)), DMA((3,)), DMA((3, 5)),
        ],
        compiler_params=pltpu.CompilerParams(
            collective_id=0, has_side_effects=True, vmem_limit_bytes=62 * 2 ** 20
        ),
        name="layer",
    )(tokens, expert_ids.T, gate_weights.T, sort, expand, lanes, w_gate[0], w_up[0], w_down[0], turn)
    return out


def solution(mesh):
    spec = P(("group", "local"), None)
    wide = P(("group", "local"), None, None)
    return jax.shard_map(
        body, mesh=mesh, in_specs=(spec, spec, spec, wide, wide, wide), out_specs=spec, check_vma=False
    )
```

```python
import jax
import jax.numpy as jnp
import numpy as np
from jax import lax
from jax.experimental import pallas as pl
from jax.experimental.pallas import tpu as pltpu
from jax.sharding import PartitionSpec as P

CAP = 10
SIDE = 4
CORES = 2
BLOCK = SIDE * CAP
SLOTS = SIDE * CORES * BLOCK
HALF = SIDE * SIDE * BLOCK
ORDERS = ((0, 1, 2), (1, 2, 0), (2, 0, 1))
WIDTHS = (1152, 1280, 1152)
STARTS = (0, 1152, 2432)
TILES = (384, 256, 384)
RING = (1, 3, 2)
PIECES = (((0, 384), (384, 768)), ((0, 512), (512, 768)), ((0, 384), (384, 768)))
CUTS = (((0, 512), (512, 640)), ((0, 512), (512, 768)), ((0, 512), (512, 640)))
BF16 = jnp.bfloat16
F32 = jnp.float32


def whereabouts():
    group, local = lax.axis_index("group"), lax.axis_index("local")
    return (group // SIDE, group % SIDE, local // CORES), local % CORES


def device_at(pos, core):
    return (pos[0] * SIDE + pos[1], pos[2] * CORES + core)


def along(pos, axis, value):
    return tuple(value if a == axis else pos[a] for a in range(3))


def greet(pos, core):
    barrier = pltpu.get_barrier_semaphore()
    peers = [device_at(pos, 1 - core)]
    for axis in range(3):
        for step in RING:
            for other in range(CORES):
                there = along(pos, axis, (pos[axis] + step) % SIDE)
                peers.append(device_at(there, (core + other) % CORES))
    for peer in peers:
        pl.semaphore_signal(barrier, inc=1, device_id=peer, device_id_type=pl.DeviceIdType.MESH)
    pl.semaphore_wait(barrier, len(peers))


def send(src, dst, send_sem, recv_sem, device):
    return pltpu.make_async_remote_copy(
        src_ref=src, dst_ref=dst, send_sem=send_sem, recv_sem=recv_sem,
        device_id=device, device_id_type=pl.DeviceIdType.MESH,
    )


def layer_kernel(tok, ids, amounts, sort, expand, lanes, wg, wu, wd, turn, out, ra, rb, rc, la, lb, lc, ha, hb, hc,
                 ga, gb, gc, sa, sb, sc, xa, xb, xc, qa, qb, qc, gate_w, up_w, down_w, turns, full, hid, hid_t, raw, tables, notes, mixed,
                 wsem, s1, r1, sm, rm, s2, r2, s3, r3, keep, t3, u3, keep_t, t2, u2, fetch, t1, u1):
    pos, core = whereabouts()
    gathered, cut, relay, held = (ga, gb, gc), (sa, sb, sc), (ra, rb, rc), (xa, xb, xc)
    landed, home, others = (la, lb, lc), (ha, hb, hc), (qa, qb, qc)
    loads = [
        pltpu.make_async_copy(a, b, wsem.at[i])
        for i, (a, b) in enumerate(((turn, turns), (wg, gate_w), (wu, up_w), (wd, down_w)))
    ]
    for copy in loads:
        copy.start()
    greet(pos, core)

    def spot(p, stage, step):
        return (pos[ORDERS[p][stage]] + step) % SIDE

    def mine(p, stage):
        return pos[ORDERS[p][stage]]

    def peer(p, stage, step, other=0):
        return device_at(along(pos, ORDERS[p][stage], spot(p, stage, step)), (core + other) % CORES)

    def tile(p, n, start=0):
        return pl.ds(pl.multiple_of(start + n * TILES[p], 128), TILES[p])

    def tables_out(p, step, slot):
        return send(tables.at[p, spot(p, 0, step)], notes.at[p, slot], sm.at[p], rm.at[p], peer(p, 0, step))

    def tokens_out(p, step, slot, piece):
        first, width = PIECES[p][piece]
        return send(
            tok.at[:, pl.ds(STARTS[p] + first, width)], gathered[p].at[slot, :, pl.ds(first, width)],
            s1.at[p], r1.at[p, slot, piece], peer(p, 0, step),
        )

    def picked_out(p, step, h, slot, piece):
        columns = pl.ds(*PIECES[p][piece])
        return send(
            cut[p].at[spot(p, 1, step), h, :, :, columns], relay[p].at[slot, h, :, :, columns],
            s2.at[p, h], r2.at[p, slot, h], peer(p, 1, step),
        )

    def block_source(p, step):
        return cut[p] if step == 0 else relay[p]

    def block_out(p, step, h, way, slot):
        origin = spot(p, 1, step)
        return send(
            block_source(p, step).at[origin, h, spot(p, 2, way)], held[p].at[h, slot, origin],
            s3.at[p, h], r3.at[p, h], peer(p, 2, way, h),
        )

    def block_kept(p, step):
        origin = spot(p, 1, step)
        return pltpu.make_async_copy(
            block_source(p, step).at[origin, 0, mine(p, 2)], held[p].at[0, mine(p, 2), origin], keep.at[p]
        )

    def result_out(p, step, h, way, slot):
        owner = spot(p, 1, step)
        return send(
            held[p].at[h, spot(p, 2, way), owner], landed[p].at[owner, h, slot],
            t3.at[p, h], u3.at[p, owner, h], peer(p, 2, way, h),
        )

    def result_kept(p, step):
        owner = spot(p, 1, step)
        return pltpu.make_async_copy(
            held[p].at[0, mine(p, 2), owner], landed[p].at[owner, 0, mine(p, 2)], keep_t.at[p, step]
        )

    def result_on(p, step, h, slot):
        return send(
            landed[p].at[spot(p, 1, step), h], home[p].at[slot, h], t2.at[p, h], u2.at[p, slot, h], peer(p, 1, step)
        )

    def fetched(p, step, h):
        origin = spot(p, 1, step)
        source = home[p] if step else landed[p]
        return pltpu.make_async_copy(source.at[origin, h], cut[p].at[origin, h], fetch.at[p])

    def sum_out(p, step, slot, n):
        columns = pl.ds(n * TILES[p], TILES[p])
        return send(
            gathered[p].at[spot(p, 0, step), :, columns], others[p].at[slot, :, columns],
            t1.at[p], u1.at[p, n], peer(p, 0, step),
        )

    def await_bytes(ref, sem):
        pltpu.make_async_copy(ref, ref, sem).wait()

    def blocks_of(p, h):
        return held[p].at[h, pl.ds(0, SIDE - 1 + h)]

    def ways(h):
        return RING + (0,) * h

    def forward(p, step, h):
        for way in ways(h):
            block_out(p, step, h, way, mine(p, 2)).start()
        if h == 0:
            block_kept(p, step).start()

    def tokens_go(piece):
        for step in RING:
            for p in range(3):
                tokens_out(p, step, mine(p, 0), piece).start()

    def tokens_come(p, piece):
        for step in RING:
            tokens_out(p, step, spot(p, 0, step), piece).wait_recv()

    def make_tables():
        rows = tok.shape[0]
        lane = lax.broadcasted_iota(jnp.int32, (rows, 128), 1)
        token = lax.broadcasted_iota(jnp.int32, (rows, 128), 0)
        named, weight = jnp.zeros((rows, 128), F32), jnp.zeros((rows, 128), F32)
        experts, worths = ids[...].astype(F32).T, amounts[...].T
        for k in range(ids.shape[0]):
            hit = experts[:, k:k + 1] == lane.astype(F32)
            named = jnp.where(hit, 1.0, named)
            weight = jnp.where(hit, worths[:, k:k + 1], weight)
        before = jnp.dot((token > lane).astype(BF16), named.astype(BF16), preferred_element_type=F32)
        place = jnp.where(named > 0.0, before, -1.0)
        number = token.astype(F32) + 1.0
        slot = lax.broadcasted_iota(jnp.int32, (16, 128), 0)
        held_by, worth = jnp.zeros((16, 128), F32), jnp.zeros((16, 128), F32)
        for s in range(CAP):
            here = place == float(s)
            held_by = jnp.where(slot == s, jnp.max(jnp.where(here, number, 0.0), axis=0, keepdims=True), held_by)
            worth = jnp.where(slot == s, jnp.sum(jnp.where(here, weight, 0.0), axis=0, keepdims=True), worth)
        for p in range(3):
            raw[...] = jnp.zeros_like(raw)
            raw[pl.ds(pl.multiple_of(16 * mine(p, 0), 16), 16), :] = held_by
            raw[pl.ds(pl.multiple_of(64 + 16 * mine(p, 0), 16), 16), :] = worth
            sorted_rows = lax.dot_general(
                sort[p], raw[...].astype(BF16), (((1,), (1,)), ((), ())), preferred_element_type=F32
            )
            tables[p] = sorted_rows.astype(BF16).reshape(SIDE, 32, 128)

    def slot_columns(p, h):
        merged = notes[p, 0].astype(F32)
        for k in range(1, SIDE):
            merged = merged + notes[p, k].astype(F32)
        wide = jnp.dot(expand[(core + h) % CORES], merged.astype(BF16), preferred_element_type=F32)
        group = lax.broadcasted_iota(jnp.int32, (1, 128), 1) // 16 * 128
        own = wide * lanes[0].astype(F32)
        index = jnp.sum(own + jnp.where(own > 0.0, group.astype(F32), 0.0), axis=1, keepdims=True) - 1.0
        return index, jnp.sum(wide * lanes[1].astype(F32), axis=1, keepdims=True)

    def find(p, h):
        first = (2 * p + h) * 512
        place = lax.broadcasted_iota(jnp.int32, (HALF, SIDE * 128), 1).astype(F32)
        full[:, first:first + 512] = (slot_columns(p, h)[0] == place).astype(BF16)

    def turn_columns(p, h):
        index, weight = slot_columns(p, h)
        lane = lax.broadcasted_iota(jnp.int32, (HALF, 128), 1)
        mixed[p, h] = jnp.where(lane == 0, index, jnp.where(lane == 1, weight, 0.0)).T[:8]

    def pick(p, h, piece):
        first = (2 * p + h) * 512
        start, width = PIECES[p][piece]

        @pl.loop(0, width // TILES[p])
        def _(n):
            columns = tile(p, n, start)
            rows = gathered[p][:, :, columns].reshape(SIDE * 128, TILES[p])
            found = jnp.dot(full[:, first:first + 512], rows, preferred_element_type=F32)
            for b in range(SIDE * SIDE):
                block = found[b * BLOCK:(b + 1) * BLOCK].astype(BF16)
                cut[p][b // SIDE, h, b % SIDE, :, columns] = block

    with jax.named_scope("send_tokens"):
        tokens_go(0)
        make_tables()
        for step in RING:
            for p in range(3):
                tables_out(p, step, mine(p, 0)).start()
        tokens_go(1)
        for p in range(3):
            gathered[p][mine(p, 0)] = tok[:, STARTS[p]:STARTS[p] + WIDTHS[p]]
            notes[p, mine(p, 0)] = tables[p, mine(p, 0)]

    with jax.named_scope("pick_rows"):
        for p in range(3):
            await_bytes(notes.at[p, pl.ds(0, SIDE - 1)], rm.at[p])
            find(p, 0)
        for piece in range(2):
            for p in range(3):
                tokens_come(p, piece)
                pick(p, 0, piece)
                for step in RING:
                    picked_out(p, step, 0, mine(p, 1), piece).start()
                if piece == 1:
                    forward(p, 0, 0)
        for p in range(3):
            find(p, 1)
            for piece in range(2):
                pick(p, 1, piece)

    with jax.named_scope("relay_rows"):
        for at, step in enumerate((3, 1, 2)):
            for p in range(3):
                await_bytes(relay[p].at[spot(p, 1, step), 0], r2.at[p, spot(p, 1, step), 0])
                forward(p, step, 0)
                for piece in range(2):
                    picked_out(p, RING[at], 1, mine(p, 1), piece).start()
        for p in range(3):
            forward(p, 0, 1)
        for p in range(3):
            for h in range(CORES):
                turn_columns(p, h)

    def relay_rows(step):
        for p in range(3):
            await_bytes(relay[p].at[spot(p, 1, step), 1], r2.at[p, spot(p, 1, step), 1])
            forward(p, step, 1)

    def relay_results(step, h):
        for p in range(3):
            landing(p, step, h)
            result_on(p, step, h, mine(p, 1)).start()

    def arrive(p, h):
        await_bytes(blocks_of(p, h), r3.at[p, h])
        if h == 0:
            await_bytes(held[p].at[0, 0], keep.at[p])

    def line_up(h):
        for p in range(3):
            arrive(p, h)
            for start, width in CUTS[p]:
                columns = slice(start, start + width)
                rows = held[p][h, :, :, :, columns].astype(F32).reshape(HALF, width).astype(BF16)
                if p != 1:
                    rows = jnp.dot(turns[p // 2], rows, preferred_element_type=F32).astype(BF16)
                full[:, STARTS[p] + start:STARTS[p] + start + width] = rows

    def hide(between):
        for n in range(2):
            columns = slice(n * 512, (n + 1) * 512)
            gate = jnp.dot(full[...], gate_w[:, columns], preferred_element_type=F32)
            between(2 * n)
            lin = jnp.dot(full[...], up_w[:, columns], preferred_element_type=F32)
            hid[:, columns] = (gate * (1.0 / (1.0 + jnp.exp(-gate))) * lin).astype(BF16)
            if n == 0:
                between(1)

    def answer(h, p):
        rows = hid if p == 1 else hid_t
        if p != 1:
            @pl.loop(0, 4)
            def _(n):
                columns = pl.ds(pl.multiple_of(n * 256, 128), 256)
                hid_t[:, columns] = jnp.dot(turns[1 - p // 2], hid[:, columns], preferred_element_type=F32).astype(BF16)

        for start, width in CUTS[p]:
            of_w = slice(STARTS[p] + start, STARTS[p] + start + width)
            result = jnp.dot(rows[...], down_w[:, of_w], preferred_element_type=F32)
            for b in range(SIDE * SIDE):
                block = result[b * BLOCK:(b + 1) * BLOCK].astype(BF16)
                held[p][h, b // SIDE, b % SIDE, :, start:start + width] = block

        for step in RING + (0,):
            for way in ways(h):
                result_out(p, step, h, way, mine(p, 2)).start()
            if h == 0:
                result_kept(p, step).start()

    def landing(p, step, h):
        owner = spot(p, 1, step)
        await_bytes(landed[p].at[owner, h, pl.ds(0, SIDE - 1 + h)], u3.at[p, owner, h])
        if h == 0:
            result_kept(p, step).wait()

    with jax.named_scope("line_up"):
        loads[0].wait()
        line_up(0)
    with jax.named_scope("hidden"):
        loads[1].wait()
        loads[2].wait()
        hide(lambda n: relay_rows((3, 1, 2)[n]))
    with jax.named_scope("answer"):
        loads[3].wait()
        for p in (1, 0, 2):
            answer(0, p)
    with jax.named_scope("line_up"):
        line_up(1)
    with jax.named_scope("hidden"):
        hide(lambda n: relay_results(RING[n], 0))
    with jax.named_scope("answer"):
        for p in (1, 0, 2):
            answer(1, p)
    with jax.named_scope("wait_sent"):
        for p in range(3):
            await_bytes(notes.at[p, pl.ds(0, SIDE - 1)], sm.at[p])
            await_bytes(gathered[p].at[pl.ds(0, SIDE - 1)], s1.at[p])
            for h in range(CORES):
                await_bytes(blocks_of(p, 0), s2.at[p, h])
                await_bytes(blocks_of(p, h), s3.at[p, h])
    with jax.named_scope("fetch_own"):
        for p in range(3):
            landing(p, 0, 0)
            fetched(p, 0, 0).start()
        for step in (3, 1, 2):
            for p in range(3):
                result_on(p, step, 0, spot(p, 1, step)).wait_recv()
                fetched(p, step, 0).start()
    with jax.named_scope("relay_results_other"):
        for step in RING:
            relay_results(step, 1)
        for p in range(3):
            landing(p, 0, 1)
            fetched(p, 0, 1).start()

    def spread(p, h):
        if p < 2:
            return full, slice((2 * p + h) * HALF, (2 * p + h + 1) * HALF)
        return (hid, hid_t)[h], slice(0, HALF)

    with jax.named_scope("spread_weights"):
        token = lax.broadcasted_iota(jnp.int32, (SIDE * 128, HALF), 0).astype(F32)
        for p in range(3):
            for h in range(CORES):
                ref, columns = spread(p, h)
                ref[:SIDE * 128, columns] = jnp.where(token == mixed[p, h, 0:1], mixed[p, h, 1:2], 0.0).astype(BF16)
    with jax.named_scope("weighted_sum"):
        for step in (3, 1, 2):
            for p in range(3):
                result_on(p, step, 1, spot(p, 1, step)).wait_recv()
                fetched(p, step, 1).start()
        for n in range(max(w // t for w, t in zip(WIDTHS, TILES))):
            for p in range(3):
                if n >= WIDTHS[p] // TILES[p]:
                    continue
                if n == 0:
                    await_bytes(cut[p], fetch.at[p])
                columns = slice(n * TILES[p], (n + 1) * TILES[p])
                total = jnp.zeros((SIDE * 128, TILES[p]), F32)
                for h in range(CORES):
                    rows = cut[p][:, h, :, :, columns].astype(F32).reshape(HALF, TILES[p]).astype(BF16)
                    ref, of_slots = spread(p, h)
                    total = total + jnp.dot(ref[:SIDE * 128, of_slots], rows, preferred_element_type=F32)
                for k in range(SIDE):
                    gathered[p][k, :, columns] = total[k * 128:(k + 1) * 128].astype(BF16)
                for step in RING:
                    sum_out(p, step, mine(p, 0), n).start()
    with jax.named_scope("last_sum"):
        for n in range(max(w // t for w, t in zip(WIDTHS, TILES))):
            for p in range(3):
                if n >= WIDTHS[p] // TILES[p]:
                    continue
                columns = slice(n * TILES[p], (n + 1) * TILES[p])
                total = gathered[p][mine(p, 0), :, columns].astype(F32)
                await_bytes(others[p].at[pl.ds(0, SIDE - 1), :, columns], u1.at[p, n])
                for step in RING:
                    total = total + others[p][spot(p, 0, step), :, columns].astype(F32)
                out[:, STARTS[p] + n * TILES[p]:STARTS[p] + (n + 1) * TILES[p]] = total.astype(BF16)
    for p in range(3):
        await_bytes(gathered[p].at[pl.ds(0, SIDE - 1)], t1.at[p])
        for h in range(CORES):
            await_bytes(blocks_of(p, 0), t2.at[p, h])
            await_bytes(blocks_of(p, h), t3.at[p, h])


ANY = pl.BlockSpec(memory_space=pl.ANY)
VMEM = pl.BlockSpec(memory_space=pltpu.VMEM)
DMA = pltpu.SemaphoreType.DMA


def blocks(leading):
    return [jax.ShapeDtypeStruct(leading + (w,), BF16) for w in WIDTHS]


def scratch(leading):
    return [pltpu.VMEM(leading + (w,), BF16) for w in WIDTHS]


def constants():
    row = np.arange(HALF)
    k, i, j, s = row // 160, row // 40 % 4, row // 10 % 4, row % 10
    there = (i * 160 + j * 40 + k * 10 + s)[:, None] == row[None, :]
    turn = np.stack([there, there.T])
    expert = np.arange(SIDE ** 3 * CORES).reshape(SIDE, SIDE, SIDE, CORES)
    sort = np.stack([expert.transpose(*order, 3).reshape(-1)[:, None] == np.arange(expert.size) for order in ORDERS])
    expand = np.stack([((row // 40) * CORES + core)[:, None] == np.arange(32) for core in range(CORES)])
    lane = (j * 16 + s)[:, None]
    lanes = np.stack([lane == np.arange(128), lane + 64 == np.arange(128)])
    return tuple(jnp.asarray(a.astype(np.float32), dtype=BF16) for a in (sort, expand, lanes, turn))


def body(tokens, expert_ids, gate_weights, w_gate, w_up, w_down):
    sort, expand, lanes, turn = constants()
    split = (SIDE, CORES, SIDE, BLOCK)
    out, *_ = pl.pallas_call(
        layer_kernel,
        out_shape=[jax.ShapeDtypeStruct(tokens.shape, BF16)] + blocks(split) * 3,
        in_specs=[VMEM] * 6 + [ANY] * 4,
        out_specs=[VMEM] + [ANY] * 9,
        scratch_shapes=scratch((SIDE, 128)) + scratch(split) + scratch((CORES, SIDE, SIDE, BLOCK)) + scratch((SIDE, 128)) + [
            pltpu.VMEM(w_gate.shape[1:], BF16), pltpu.VMEM(w_up.shape[1:], BF16), pltpu.VMEM(w_down.shape[1:], BF16),
            pltpu.VMEM((2, HALF, HALF), BF16),
            pltpu.VMEM((HALF, tokens.shape[1]), BF16),
            pltpu.VMEM((HALF, w_gate.shape[2]), BF16),
            pltpu.VMEM((HALF, w_gate.shape[2]), BF16),
            pltpu.VMEM((128, 128), F32),
            pltpu.VMEM((3, SIDE, 32, 128), BF16),
            pltpu.VMEM((3, SIDE, 32, 128), BF16),
            pltpu.VMEM((3, CORES, 8, HALF), F32),
        ] + [
            DMA((4,)), DMA((3,)), DMA((3, SIDE, 2)), DMA((3,)), DMA((3,)),
            DMA((3, CORES)), DMA((3, SIDE, CORES)), DMA((3, CORES)), DMA((3, CORES)), DMA((3,)),
            DMA((3, CORES)), DMA((3, SIDE, CORES)), DMA((3, SIDE)), DMA((3, CORES)), DMA((3, SIDE, CORES)),
            DMA((3,)), DMA((3,)), DMA((3, 5)),
        ],
        compiler_params=pltpu.CompilerParams(
            collective_id=0, has_side_effects=True, vmem_limit_bytes=62 * 2 ** 20
        ),
        name="layer",
    )(tokens, expert_ids.T, gate_weights.T, sort, expand, lanes, w_gate[0], w_up[0], w_down[0], turn)
    return out


def solution(mesh):
    spec = P(("group", "local"), None)
    wide = P(("group", "local"), None, None)
    return jax.shard_map(
        body, mesh=mesh, in_specs=(spec, spec, spec, wide, wide, wide), out_specs=spec, check_vma=False
    )
```

```python
import jax
import jax.numpy as jnp
import numpy as np
from jax import lax
from jax.experimental import pallas as pl
from jax.experimental.pallas import tpu as pltpu
from jax.sharding import PartitionSpec as P

CAP = 10
SIDE = 4
CORES = 2
BLOCK = SIDE * CAP
SLOTS = SIDE * CORES * BLOCK
HALF = SIDE * SIDE * BLOCK
ORDERS = ((0, 1, 2), (1, 2, 0), (2, 0, 1))
WIDTHS = (1152, 1280, 1152)
STARTS = (0, 1152, 2432)
RING = (1, 3, 2)
CUTS = (((0, 512), (512, 640)), ((0, 512), (512, 768)), ((0, 512), (512, 640)))
BF16 = jnp.bfloat16
F32 = jnp.float32


def whereabouts():
    group, local = lax.axis_index("group"), lax.axis_index("local")
    return (group // SIDE, group % SIDE, local // CORES), local % CORES


def device_at(pos, core):
    return (pos[0] * SIDE + pos[1], pos[2] * CORES + core)


def along(pos, axis, value):
    return tuple(value if a == axis else pos[a] for a in range(3))


def greet(pos, core):
    barrier = pltpu.get_barrier_semaphore()
    peers = [device_at(pos, 1 - core)]
    for axis in range(3):
        for step in RING:
            for other in range(CORES):
                there = along(pos, axis, (pos[axis] + step) % SIDE)
                peers.append(device_at(there, (core + other) % CORES))
    for peer in peers:
        pl.semaphore_signal(barrier, inc=1, device_id=peer, device_id_type=pl.DeviceIdType.MESH)
    pl.semaphore_wait(barrier, len(peers))


def send(src, dst, send_sem, recv_sem, device):
    return pltpu.make_async_remote_copy(
        src_ref=src, dst_ref=dst, send_sem=send_sem, recv_sem=recv_sem,
        device_id=device, device_id_type=pl.DeviceIdType.MESH,
    )


def layer_kernel(tok, ids, amounts, sort, expand, lanes, wg, wu, wd, turn, out, ra, rb, rc, la, lb, lc, ha, hb, hc,
                 ga, gb, gc, sa, sb, sc, xa, xb, xc, qa, qb, qc, gate_w, up_w, down_w, turns, full, hid, hid_t, raw, tables, notes, mixed,
                 wsem, s1, r1, sm, rm, s2, r2, s3, r3, keep, t3, u3, keep_t, t2, u2, fetch, t1, u1):
    pos, core = whereabouts()
    gathered, cut, relay, held = (ga, gb, gc), (sa, sb, sc), (ra, rb, rc), (xa, xb, xc)
    landed, home, others = (la, lb, lc), (ha, hb, hc), (qa, qb, qc)
    loads = [
        pltpu.make_async_copy(a, b, wsem.at[i])
        for i, (a, b) in enumerate(((turn, turns), (wg, gate_w), (wu, up_w), (wd, down_w)))
    ]
    for copy in loads:
        copy.start()
    greet(pos, core)

    def spot(p, stage, step):
        return (pos[ORDERS[p][stage]] + step) % SIDE

    def mine(p, stage):
        return pos[ORDERS[p][stage]]

    def peer(p, stage, step, other=0):
        return device_at(along(pos, ORDERS[p][stage], spot(p, stage, step)), (core + other) % CORES)

    def tables_out(p, step, slot):
        return send(tables.at[p, spot(p, 0, step)], notes.at[p, slot], sm.at[p], rm.at[p], peer(p, 0, step))

    def tokens_out(p, step, slot, piece):
        first, width = CUTS[p][piece]
        return send(
            tok.at[:, pl.ds(STARTS[p] + first, width)], gathered[p].at[slot, :, pl.ds(first, width)],
            s1.at[p], r1.at[p, slot, piece], peer(p, 0, step),
        )

    def picked_out(p, step, h, slot, piece):
        columns = pl.ds(*CUTS[p][piece])
        return send(
            cut[p].at[spot(p, 1, step), h, :, :, columns], relay[p].at[slot, h, :, :, columns],
            s2.at[p, h], r2.at[p, slot, h], peer(p, 1, step),
        )

    def block_source(p, step):
        return cut[p] if step == 0 else relay[p]

    def block_out(p, step, h, way, slot):
        origin = spot(p, 1, step)
        return send(
            block_source(p, step).at[origin, h, spot(p, 2, way)], held[p].at[h, slot, origin],
            s3.at[p, h], r3.at[p, h], peer(p, 2, way, h),
        )

    def block_kept(p, step):
        origin = spot(p, 1, step)
        return pltpu.make_async_copy(
            block_source(p, step).at[origin, 0, mine(p, 2)], held[p].at[0, mine(p, 2), origin], keep.at[p]
        )

    def result_out(p, step, h, way, slot):
        owner = spot(p, 1, step)
        return send(
            held[p].at[h, spot(p, 2, way), owner], landed[p].at[owner, h, slot],
            t3.at[p, h], u3.at[p, owner, h], peer(p, 2, way, h),
        )

    def result_kept(p, step):
        owner = spot(p, 1, step)
        return pltpu.make_async_copy(
            held[p].at[0, mine(p, 2), owner], landed[p].at[owner, 0, mine(p, 2)], keep_t.at[p, step]
        )

    def result_on(p, step, h, slot):
        return send(
            landed[p].at[spot(p, 1, step), h], home[p].at[slot, h], t2.at[p, h], u2.at[p, slot, h], peer(p, 1, step)
        )

    def fetched(p, step, h):
        origin = spot(p, 1, step)
        source = home[p] if step else landed[p]
        return pltpu.make_async_copy(source.at[origin, h], cut[p].at[origin, h], fetch.at[p])

    def sum_out(p, step, slot, n):
        columns = pl.ds(*CUTS[p][n])
        return send(
            gathered[p].at[spot(p, 0, step), :, columns], others[p].at[slot, :, columns],
            t1.at[p], u1.at[p, n], peer(p, 0, step),
        )

    def await_bytes(ref, sem):
        pltpu.make_async_copy(ref, ref, sem).wait()

    def blocks_of(p, h):
        return held[p].at[h, pl.ds(0, SIDE - 1 + h)]

    def ways(h):
        return RING + (0,) * h

    def forward(p, step, h):
        for way in ways(h):
            block_out(p, step, h, way, mine(p, 2)).start()
        if h == 0:
            block_kept(p, step).start()

    def tokens_go(piece):
        for step in RING:
            for p in range(3):
                tokens_out(p, step, mine(p, 0), piece).start()

    def tokens_come(p, piece):
        for step in RING:
            tokens_out(p, step, spot(p, 0, step), piece).wait_recv()

    def make_tables():
        rows = tok.shape[0]
        lane = lax.broadcasted_iota(jnp.int32, (rows, 128), 1)
        token = lax.broadcasted_iota(jnp.int32, (rows, 128), 0)
        named, weight = jnp.zeros((rows, 128), F32), jnp.zeros((rows, 128), F32)
        experts, worths = ids[...].astype(F32).T, amounts[...].T
        for k in range(ids.shape[0]):
            hit = experts[:, k:k + 1] == lane.astype(F32)
            named = jnp.where(hit, 1.0, named)
            weight = jnp.where(hit, worths[:, k:k + 1], weight)
        before = jnp.dot((token > lane).astype(BF16), named.astype(BF16), preferred_element_type=F32)
        place = jnp.where(named > 0.0, before, -1.0)
        number = token.astype(F32) + 1.0
        slot = lax.broadcasted_iota(jnp.int32, (16, 128), 0)
        held_by, worth = jnp.zeros((16, 128), F32), jnp.zeros((16, 128), F32)
        for s in range(CAP):
            here = place == float(s)
            held_by = jnp.where(slot == s, jnp.max(jnp.where(here, number, 0.0), axis=0, keepdims=True), held_by)
            worth = jnp.where(slot == s, jnp.sum(jnp.where(here, weight, 0.0), axis=0, keepdims=True), worth)
        for p in range(3):
            raw[...] = jnp.zeros_like(raw)
            raw[pl.ds(pl.multiple_of(16 * mine(p, 0), 16), 16), :] = held_by
            raw[pl.ds(pl.multiple_of(64 + 16 * mine(p, 0), 16), 16), :] = worth
            sorted_rows = lax.dot_general(
                sort[p], raw[...].astype(BF16), (((1,), (1,)), ((), ())), preferred_element_type=F32
            )
            tables[p] = sorted_rows.astype(BF16).reshape(SIDE, 32, 128)

    def slot_columns(p, h):
        merged = notes[p, 0].astype(F32)
        for k in range(1, SIDE):
            merged = merged + notes[p, k].astype(F32)
        wide = jnp.dot(expand[(core + h) % CORES], merged.astype(BF16), preferred_element_type=F32)
        group = lax.broadcasted_iota(jnp.int32, (1, 128), 1) // 16 * 128
        own = wide * lanes[0].astype(F32)
        index = jnp.sum(own + jnp.where(own > 0.0, group.astype(F32), 0.0), axis=1, keepdims=True) - 1.0
        return index, jnp.sum(wide * lanes[1].astype(F32), axis=1, keepdims=True)

    def find(p, h):
        first = (2 * p + h) * 512
        place = lax.broadcasted_iota(jnp.int32, (HALF, SIDE * 128), 1).astype(F32)
        full[:, first:first + 512] = (slot_columns(p, h)[0] == place).astype(BF16)

    def turn_columns(p, h):
        index, weight = slot_columns(p, h)
        lane = lax.broadcasted_iota(jnp.int32, (HALF, 128), 1)
        mixed[p, h] = jnp.where(lane == 0, index, jnp.where(lane == 1, weight, 0.0)).T[:8]

    def pick(p, h, piece):
        first = (2 * p + h) * 512
        start, width = CUTS[p][piece]
        columns = slice(start, start + width)
        rows = gathered[p][:, :, columns].reshape(SIDE * 128, width)
        found = jnp.dot(full[:, first:first + 512], rows, preferred_element_type=F32)
        for b in range(SIDE * SIDE):
            cut[p][b // SIDE, h, b % SIDE, :, columns] = found[b * BLOCK:(b + 1) * BLOCK].astype(BF16)

    with jax.named_scope("send_tokens"):
        tokens_go(0)
        make_tables()
        for step in RING:
            for p in range(3):
                tables_out(p, step, mine(p, 0)).start()
        tokens_go(1)
        for p in range(3):
            gathered[p][mine(p, 0)] = tok[:, STARTS[p]:STARTS[p] + WIDTHS[p]]
            notes[p, mine(p, 0)] = tables[p, mine(p, 0)]

    with jax.named_scope("pick_rows"):
        for p in range(3):
            await_bytes(notes.at[p, pl.ds(0, SIDE - 1)], rm.at[p])
            find(p, 0)
        for piece in range(2):
            for p in range(3):
                tokens_come(p, piece)
                pick(p, 0, piece)
                for step in RING:
                    picked_out(p, step, 0, mine(p, 1), piece).start()
                if piece == 1:
                    forward(p, 0, 0)
        for p in range(3):
            find(p, 1)
            for piece in range(2):
                pick(p, 1, piece)

    with jax.named_scope("relay_rows"):
        for at, step in enumerate((3, 1, 2)):
            for p in range(3):
                await_bytes(relay[p].at[spot(p, 1, step), 0], r2.at[p, spot(p, 1, step), 0])
                forward(p, step, 0)
                for piece in range(2):
                    picked_out(p, RING[at], 1, mine(p, 1), piece).start()
        for p in range(3):
            forward(p, 0, 1)
        for p in range(3):
            for h in range(CORES):
                turn_columns(p, h)

    def relay_rows(step):
        for p in range(3):
            await_bytes(relay[p].at[spot(p, 1, step), 1], r2.at[p, spot(p, 1, step), 1])
            forward(p, step, 1)

    def relay_results(step, h):
        for p in range(3):
            landing(p, step, h)
            result_on(p, step, h, mine(p, 1)).start()

    def arrive(p, h):
        await_bytes(blocks_of(p, h), r3.at[p, h])
        if h == 0:
            await_bytes(held[p].at[0, 0], keep.at[p])

    def line_up(h):
        for p in range(3):
            arrive(p, h)
            for start, width in CUTS[p]:
                columns = slice(start, start + width)
                rows = held[p][h, :, :, :, columns].astype(F32).reshape(HALF, width).astype(BF16)
                if p != 1:
                    rows = jnp.dot(turns[p // 2], rows, preferred_element_type=F32).astype(BF16)
                full[:, STARTS[p] + start:STARTS[p] + start + width] = rows

    def hide(between):
        for n in range(2):
            columns = slice(n * 512, (n + 1) * 512)
            gate = jnp.dot(full[...], gate_w[:, columns], preferred_element_type=F32)
            between(2 * n)
            lin = jnp.dot(full[...], up_w[:, columns], preferred_element_type=F32)
            hid[:, columns] = (gate * (1.0 / (1.0 + jnp.exp(-gate))) * lin).astype(BF16)
            if n == 0:
                between(1)

    def answer(h, p):
        rows = hid if p == 1 else hid_t
        if p != 1:
            @pl.loop(0, 4)
            def _(n):
                columns = pl.ds(pl.multiple_of(n * 256, 128), 256)
                hid_t[:, columns] = jnp.dot(turns[1 - p // 2], hid[:, columns], preferred_element_type=F32).astype(BF16)

        for start, width in CUTS[p]:
            of_w = slice(STARTS[p] + start, STARTS[p] + start + width)
            result = jnp.dot(rows[...], down_w[:, of_w], preferred_element_type=F32)
            for b in range(SIDE * SIDE):
                block = result[b * BLOCK:(b + 1) * BLOCK].astype(BF16)
                held[p][h, b // SIDE, b % SIDE, :, start:start + width] = block

        for step in RING + (0,):
            for way in ways(h):
                result_out(p, step, h, way, mine(p, 2)).start()
            if h == 0:
                result_kept(p, step).start()

    def landing(p, step, h):
        owner = spot(p, 1, step)
        await_bytes(landed[p].at[owner, h, pl.ds(0, SIDE - 1 + h)], u3.at[p, owner, h])
        if h == 0:
            result_kept(p, step).wait()

    with jax.named_scope("line_up"):
        loads[0].wait()
        line_up(0)
    with jax.named_scope("hidden"):
        loads[1].wait()
        loads[2].wait()
        hide(lambda n: relay_rows((3, 1, 2)[n]))
    with jax.named_scope("answer"):
        loads[3].wait()
        for p in (1, 0, 2):
            answer(0, p)
    with jax.named_scope("line_up"):
        line_up(1)
    with jax.named_scope("hidden"):
        hide(lambda n: relay_results(RING[n], 0))
    with jax.named_scope("answer"):
        for p in (1, 0, 2):
            answer(1, p)
    with jax.named_scope("wait_sent"):
        for p in range(3):
            await_bytes(notes.at[p, pl.ds(0, SIDE - 1)], sm.at[p])
            await_bytes(gathered[p].at[pl.ds(0, SIDE - 1)], s1.at[p])
            for h in range(CORES):
                await_bytes(blocks_of(p, 0), s2.at[p, h])
                await_bytes(blocks_of(p, h), s3.at[p, h])
    with jax.named_scope("fetch_own"):
        for p in range(3):
            landing(p, 0, 0)
            fetched(p, 0, 0).start()
        for step in (3, 1, 2):
            for p in range(3):
                result_on(p, step, 0, spot(p, 1, step)).wait_recv()
                fetched(p, step, 0).start()
    with jax.named_scope("relay_results_other"):
        for step in RING:
            relay_results(step, 1)
        for p in range(3):
            landing(p, 0, 1)
            fetched(p, 0, 1).start()

    def spread(p, h):
        if p < 2:
            return full, slice((2 * p + h) * HALF, (2 * p + h + 1) * HALF)
        return (hid, hid_t)[h], slice(0, HALF)

    with jax.named_scope("spread_weights"):
        token = lax.broadcasted_iota(jnp.int32, (SIDE * 128, HALF), 0).astype(F32)
        for p in range(3):
            for h in range(CORES):
                ref, columns = spread(p, h)
                ref[:SIDE * 128, columns] = jnp.where(token == mixed[p, h, 0:1], mixed[p, h, 1:2], 0.0).astype(BF16)
    with jax.named_scope("weighted_sum"):
        for step in (3, 1, 2):
            for p in range(3):
                result_on(p, step, 1, spot(p, 1, step)).wait_recv()
                fetched(p, step, 1).start()
        for n in range(2):
            for p in range(3):
                if n == 0:
                    await_bytes(cut[p], fetch.at[p])
                start, width = CUTS[p][n]
                columns = slice(start, start + width)
                total = jnp.zeros((SIDE * 128, width), F32)
                for h in range(CORES):
                    rows = cut[p][:, h, :, :, columns].astype(F32).reshape(HALF, width).astype(BF16)
                    ref, of_slots = spread(p, h)
                    total = total + jnp.dot(ref[:SIDE * 128, of_slots], rows, preferred_element_type=F32)
                for k in range(SIDE):
                    gathered[p][k, :, columns] = total[k * 128:(k + 1) * 128].astype(BF16)
                for step in RING:
                    sum_out(p, step, mine(p, 0), n).start()
    with jax.named_scope("last_sum"):
        for n in range(2):
            for p in range(3):
                start, width = CUTS[p][n]
                columns = slice(start, start + width)
                total = gathered[p][mine(p, 0), :, columns].astype(F32)
                await_bytes(others[p].at[pl.ds(0, SIDE - 1), :, columns], u1.at[p, n])
                for step in RING:
                    total = total + others[p][spot(p, 0, step), :, columns].astype(F32)
                out[:, STARTS[p] + start:STARTS[p] + start + width] = total.astype(BF16)
    for p in range(3):
        await_bytes(gathered[p].at[pl.ds(0, SIDE - 1)], t1.at[p])
        for h in range(CORES):
            await_bytes(blocks_of(p, 0), t2.at[p, h])
            await_bytes(blocks_of(p, h), t3.at[p, h])


ANY = pl.BlockSpec(memory_space=pl.ANY)
VMEM = pl.BlockSpec(memory_space=pltpu.VMEM)
DMA = pltpu.SemaphoreType.DMA


def blocks(leading):
    return [jax.ShapeDtypeStruct(leading + (w,), BF16) for w in WIDTHS]


def scratch(leading):
    return [pltpu.VMEM(leading + (w,), BF16) for w in WIDTHS]


def constants():
    row = np.arange(HALF)
    k, i, j, s = row // 160, row // 40 % 4, row // 10 % 4, row % 10
    there = (i * 160 + j * 40 + k * 10 + s)[:, None] == row[None, :]
    turn = np.stack([there, there.T])
    expert = np.arange(SIDE ** 3 * CORES).reshape(SIDE, SIDE, SIDE, CORES)
    sort = np.stack([expert.transpose(*order, 3).reshape(-1)[:, None] == np.arange(expert.size) for order in ORDERS])
    expand = np.stack([((row // 40) * CORES + core)[:, None] == np.arange(32) for core in range(CORES)])
    lane = (j * 16 + s)[:, None]
    lanes = np.stack([lane == np.arange(128), lane + 64 == np.arange(128)])
    return tuple(jnp.asarray(a.astype(np.float32), dtype=BF16) for a in (sort, expand, lanes, turn))


def body(tokens, expert_ids, gate_weights, w_gate, w_up, w_down):
    sort, expand, lanes, turn = constants()
    split = (SIDE, CORES, SIDE, BLOCK)
    out, *_ = pl.pallas_call(
        layer_kernel,
        out_shape=[jax.ShapeDtypeStruct(tokens.shape, BF16)] + blocks(split) * 3,
        in_specs=[VMEM] * 6 + [ANY] * 4,
        out_specs=[VMEM] + [ANY] * 9,
        scratch_shapes=scratch((SIDE, 128)) + scratch(split) + scratch((CORES, SIDE, SIDE, BLOCK)) + scratch((SIDE, 128)) + [
            pltpu.VMEM(w_gate.shape[1:], BF16), pltpu.VMEM(w_up.shape[1:], BF16), pltpu.VMEM(w_down.shape[1:], BF16),
            pltpu.VMEM((2, HALF, HALF), BF16),
            pltpu.VMEM((HALF, tokens.shape[1]), BF16),
            pltpu.VMEM((HALF, w_gate.shape[2]), BF16),
            pltpu.VMEM((HALF, w_gate.shape[2]), BF16),
            pltpu.VMEM((128, 128), F32),
            pltpu.VMEM((3, SIDE, 32, 128), BF16),
            pltpu.VMEM((3, SIDE, 32, 128), BF16),
            pltpu.VMEM((3, CORES, 8, HALF), F32),
        ] + [
            DMA((4,)), DMA((3,)), DMA((3, SIDE, 2)), DMA((3,)), DMA((3,)),
            DMA((3, CORES)), DMA((3, SIDE, CORES)), DMA((3, CORES)), DMA((3, CORES)), DMA((3,)),
            DMA((3, CORES)), DMA((3, SIDE, CORES)), DMA((3, SIDE)), DMA((3, CORES)), DMA((3, SIDE, CORES)),
            DMA((3,)), DMA((3,)), DMA((3, 5)),
        ],
        compiler_params=pltpu.CompilerParams(
            collective_id=0, has_side_effects=True, vmem_limit_bytes=62 * 2 ** 20
        ),
        name="layer",
    )(tokens, expert_ids.T, gate_weights.T, sort, expand, lanes, w_gate[0], w_up[0], w_down[0], turn)
    return out


def solution(mesh):
    spec = P(("group", "local"), None)
    wide = P(("group", "local"), None, None)
    return jax.shard_map(
        body, mesh=mesh, in_specs=(spec, spec, spec, wide, wide, wide), out_specs=spec, check_vma=False
    )
```
